32 devices in a mesh: member: 4 (over y, core), fsdp: 8 (over z, x).
Axes of the slice: x: 2, y: 2, z: 4, core: 2. Of those that a mesh axis runs over, the one named last changes fastest.
Arguments:
- tokens: bfloat16 [1536, 4096], P('fsdp'), may hold values from -6 to 6
- routes: int32 [1536, 2], P('fsdp'), may hold values from 0 to 3, all different within a row; in each aligned block of 192 rows (0 to 191, 192 to 383, ...) at most 144 rows name the same one
- combine: float32 [1536, 2], P('fsdp'), may hold values from 0.25 to 1
- gate_weight: bfloat16 [4, 11008, 4096], P('member', None, 'fsdp'), may hold values from -0.09375 to 0.09375
- up_weight: bfloat16 [4, 11008, 4096], P('member', None, 'fsdp'), may hold values from -0.09375 to 0.09375
- down_weight: bfloat16 [4, 11008, 4096], P('member', None, 'fsdp'), may hold values from -0.0546875 to 0.0546875
Outputs:
- mixed: bfloat16 [1536, 4096], P('fsdp', 'member')
The draws below stay inside these ranges and needn't reach their ends.
Inputs may be any that keep to these rules, and one draw needn't show every extreme that they name: `routes`: each row names two different experts. In each aligned block of 192 rows no expert is named by more than 144 rows, a bound that some block reaches.
All inputs are finite; a program needn't handle non-finite values.
Results may differ from the reference program's by a relative error of at most 0.0049.
Values may be sent and summed in bfloat16 or wider, within the bound.
No kernel may reach another device: no remote copies, remote signals or barrier semaphores. Data moves between devices by JAX's collectives and lax.ppermute only.
A program may use at most 128 MiB of HBM per device.

```python
import math
import jax
import jax.numpy as jnp
import numpy as np
from jax import lax

D = 4096
FF = 11008
TOK_DEV = 192
EXPERTS = 4
MOST = 144
TOKENS = 1536
N_FSDP = 8


def level_of(key, dims, split, smallest, high):
    factor_of, own = 1.0, jax.random.fold_in(key, 6)
    for position, parts in split:
        heights = jnp.exp(jax.random.uniform(jax.random.fold_in(own, position), (parts,), jnp.float32, smallest / len(split), high / len(split)))
        factor_of = factor_of * jnp.repeat(heights, dims[position] // parts).reshape([-1 if axis == position else 1 for axis in range(len(dims))])
    return factor_of


def assign_block(rng, own, number, rows, count, top, reach, slope):
    order = jax.random.permutation(rng, count)
    crowded, ordinary = portions_of(count, rows * top, reach, slope, True), portions_of(count, rows * top, reach, slope, False)
    places = jnp.arange(count)

    def named(lengths, offset_by):
        used = int((lengths > 0).sum())
        fixed = max(1, used // 4)
        shifted = fixed + (places - fixed + offset_by * (used - fixed)) % max(1, count - fixed)
        return jnp.zeros((count,), jnp.int32).at[order[jnp.where(places < fixed, places, shifted)]].set(jnp.asarray(lengths, jnp.int32))

    lengths = jnp.where(number % 4 == 0, named(crowded, number // 4), named(ordinary, number - number // 4 - 1))
    mixed = jax.random.permutation(jax.random.fold_in(own, 3), count)
    source_of, taker = mixed[0:count // 2 * 2:2], mixed[1:count // 2 * 2:2]
    margin = jnp.minimum(lengths[source_of] - 1, reach - lengths[taker]) // 2
    margin = jnp.where((source_of == order[0]) | (taker == order[0]) | (lengths[taker] == 0), 0, jnp.maximum(margin, 0))
    shifted = jax.random.randint(jax.random.fold_in(own, 4), (count // 2,), 0, 1 << 20) % (margin + 1)
    lengths = lengths.at[source_of].add(-shifted).at[taker].add(shifted)
    labels = jnp.searchsorted(jnp.cumsum(lengths), jnp.arange(rows * top), side="right").astype(jnp.int32)
    grid = labels.reshape(top, rows).T
    grid = grid[jax.random.permutation(jax.random.fold_in(own, 1), rows)]
    offset_by = jax.random.randint(jax.random.fold_in(own, 2), (rows, 1), 0, top)
    return jnp.take_along_axis(grid, (jnp.arange(top)[None, :] + offset_by) % top, axis=1)


def portions_of(number_of, total, bound, skew, full):
    weights = [(1 << 20) // math.isqrt(rank ** skew) + 1 for rank in range(1, number_of + 1)]
    largest = bound if full else min(bound, max(-(-total // number_of), total * weights[0] // sum(weights)))
    least = 1 if total - largest >= number_of - 1 else 0
    given, surplus = [largest] + [least] * (number_of - 1), total - largest - least * (number_of - 1)
    while surplus > 0:
        candidates = [i for i in range(1, number_of) if given[i] < largest] or [i for i in range(1, number_of) if given[i] < bound]
        mass, left = sum([weights[i] for i in candidates]), surplus
        for i in candidates:
            extra = min(bound - given[i], max(1, left * weights[i] // mass), surplus)
            given[i] = given[i] + extra
            surplus = surplus - extra
    return np.array(given)


def noise(key, shape, spread, reach, pieces=(), held_as=jnp.bfloat16):
    loudness = level_of(key, shape, pieces, -0.22, 0.18) if pieces else 1.0
    array = jax.random.normal(key, shape, jnp.float32) * spread * loudness
    return jnp.minimum(jnp.maximum(array, -reach), reach).astype(held_as)


def setup_inputs(seed: int = 0) -> dict:
    splits = jax.random.split(jax.random.key(seed), 7)
    tokens = noise(splits[0], (TOKENS, D), 1.0, 6.0, ((0, 8),))
    routes_keys = jax.random.split(jax.random.fold_in(splits[1], 1), TOKENS // TOK_DEV)
    routes_turns = jax.random.permutation(jax.random.fold_in(splits[1], 3), TOKENS // TOK_DEV)
    routes = jax.vmap(lambda own, number: assign_block(jax.random.fold_in(splits[1], 2), own, number, TOK_DEV, EXPERTS, 2, MOST, 2))(routes_keys, routes_turns).reshape((TOKENS, 2))
    combine = jnp.clip(0.25 + 0.75 * jax.random.uniform(splits[2], (TOKENS, 2), jnp.float32) ** level_of(splits[2], (TOKENS, 2), ((0, 8),), -0.2, 0.2), 0.25, 1.0)
    gate_weight = noise(splits[3], (EXPERTS, FF, D), D ** -0.5, 0.09375, ((0, 4), (2, 8)))
    up_weight = noise(splits[4], (EXPERTS, FF, D), D ** -0.5, 0.09375, ((0, 4), (2, 8)))
    down_weight = noise(splits[5], (EXPERTS, FF, D), FF ** -0.5, 0.0546875, ((0, 4), (2, 8)))
    return dict(tokens=tokens, routes=routes, combine=combine, gate_weight=gate_weight, up_weight=up_weight, down_weight=down_weight)


def reference(tokens, routes, combine, gate_weight, up_weight, down_weight):
    slot_total = N_FSDP * MOST

    def expert_pass(carry, expert):
        picked = routes == expert
        chosen = jnp.any(picked, axis=1)
        token_weight = jnp.sum(jnp.where(picked, combine, jnp.zeros_like(combine)), axis=1)
        index = jnp.nonzero(chosen, size=slot_total, fill_value=0)[0].astype(jnp.int32)
        valid = jnp.arange(slot_total, dtype=jnp.int32) < jnp.sum(chosen.astype(jnp.int32))
        rows = tokens[index]
        gate = jnp.dot(rows, gate_weight[expert].T, preferred_element_type=jnp.float32)
        upper = jnp.dot(rows, up_weight[expert].T, preferred_element_type=jnp.float32)
        hidden = (jax.nn.silu(gate) * upper).astype(jnp.bfloat16)
        output = jnp.dot(hidden, down_weight[expert], preferred_element_type=jnp.float32)
        scale = jnp.where(valid, token_weight[index], jnp.zeros_like(token_weight[index]))
        carry = carry.at[index].add(scale[:, None] * output)
        return carry, None

    start_sum = jnp.zeros((tokens.shape[0], tokens.shape[1]), jnp.float32)
    total, unused = lax.scan(expert_pass, start_sum, jnp.arange(EXPERTS, dtype=jnp.int32))
    return total.astype(jnp.bfloat16)
```

```python
import functools

import jax
import jax.numpy as jnp
from jax import lax
from jax.experimental import pallas as pl
from jax.experimental.pallas import tpu as pltpu
from jax.sharding import PartitionSpec as P

WIDTH = 256
HOP = 2
AHEAD = 3
BATCH = 2
VMEM = 58 * 1024 * 1024


def grid_of(size):
    across = 1
    while across * across * 4 <= size:
        across *= 2
    return size // across, across


def begin(src, dst, sem):
    copy = pltpu.make_async_copy(src, dst, sem)
    copy.start()
    return copy


def taker(refs):
    refs = list(refs)

    def take(count=1):
        out = refs[:count]
        del refs[:count]
        return out

    return take


def rows_at(ref, start, width):
    return ref.at[pl.ds(pl.multiple_of(start, 16), width)]


def chain_kernel(cfg, *refs):
    deep, across, width, sums, sums_in, back, back_in = cfg
    take = taker(refs)
    (info,) = take()
    if sums:
        gate, up, toks = take(3)
        got = [take(across - 1) for _ in range(deep)]
    came = take(2) if sums_in or back_in else None
    sent = take(2)
    (hid_out,) = take() if back else (None,)
    if sums:
        toks_v, w_v, tok_sem, w_sem = take(4)
    if came:
        came_v, came_sem = take(2)
    sent_v, sent_sem = take(2)
    if back:
        hid_v, hid_sem = take(2)
    place = info[0]
    odd = lax.rem(place, 2)
    wide = 2 * width if sums else 0
    in_wide = came[0].shape[1] - (width if back_in else 0) if came else 0
    half = sent[0].shape[0]
    copies = []

    waits = [[], []]
    for s in range(2):
        if came:
            for slot in range(2):

                @pl.when(lax.rem(odd + s, 2) == 1 - slot)
                def _(src=came[slot], s=s):
                    pltpu.make_async_copy(src, came_v.at[s], came_sem.at[s]).start()

            waits[s].append(pltpu.make_async_copy(came[0], came_v.at[s], came_sem.at[s]))
    if sums:
        part_rows = gate.shape[0] // across
        tok_copies = [
            begin(
                toks.at[:, pl.ds(s * half, half)],
                toks_v.at[:, pl.ds(s * half, half)],
                tok_sem.at[s],
            )
            for s in (1, 0)
        ][::-1]
        for s in range(2):
            own = info[1] * part_rows + info[2 + s]
            for k, ref in enumerate((gate, up)):
                waits[s].append(
                    begin(
                        rows_at(ref, own, width),
                        w_v.at[s, 0, pl.ds(k * width, width)],
                        w_sem.at[s, 0, k],
                    )
                )
            for j in range(1, across):
                dst, sem = w_v.at[s, j], w_sem.at[s, j, 0]
                for i in range(deep):
                    here = i if s == 0 else deep - 1 - i

                    @pl.when(place == here)
                    def _(src=got[i][j - 1], dst=dst, sem=sem):
                        pltpu.make_async_copy(src.at[pl.ds(0, 2 * width)], dst, sem).start()

                waits[s].append(
                    pltpu.make_async_copy(got[0][j - 1].at[pl.ds(0, 2 * width)], dst, sem)
                )

    ends = []
    for s in range(2):
        for copy in waits[s]:
            copy.wait()
        if not sums:
            continue
        mine = 1 - s
        tok_copies[mine].wait()
        total = None
        for j in range(across):
            term = lax.dot_general(
                toks_v[j, pl.ds(mine * half, half), :],
                w_v[s, j],
                (((1,), (1,)), ((), ())),
                preferred_element_type=jnp.float32,
            )
            total = term if total is None else total + term
        if sums_in:
            first = place == (0 if s == 0 else deep - 1)
            before = came_v[s, :, : 2 * width].astype(jnp.float32)
            total = total + jnp.where(first, 0.0, before)
        sent_v[s, :, : 2 * width] = total.astype(jnp.bfloat16)
        if back:
            value, upper = total[:, :width], total[:, width:]
            hidden = value / (1.0 + jnp.exp(-value)) * upper
            column = lax.broadcasted_iota(jnp.int32, hidden.shape, 1)
            ends.append(jnp.where(column >= info[4], hidden, 0.0).astype(jnp.bfloat16))
    if back:
        for s in range(2):
            value = came_v[s, :, in_wide:] if back_in else None
            if sums:
                at_end = place == (0 if s == 0 else deep - 1)
                other = value if back_in else jnp.zeros_like(ends[1 - s])
                value = jnp.where(at_end, ends[1 - s], other)
            sent_v[s, :, wide:] = value
            hid_v[pl.ds(s * half, half)] = value
    for s in range(2):
        for slot in range(2):

            @pl.when(lax.rem(odd + s, 2) == slot)
            def _(dst=sent[slot], s=s):
                pltpu.make_async_copy(sent_v.at[s], dst, sent_sem.at[s]).start()

        copies.append(pltpu.make_async_copy(sent_v.at[s], sent[0], sent_sem.at[s]))
    if back:
        copies.append(begin(hid_v, hid_out, hid_sem))
    for copy in copies:
        copy.wait()


def side_kernel(cfg, *refs):
    deep, across, width, steps, n_send = cfg
    take = taker(refs)
    (info,) = take()
    gate, up, down = take(3)
    hids = take(steps)
    got = [[take(across - 1) for _ in range(deep)] for _ in range(steps)]
    acc_in = take() if steps else None
    sent = take(n_send)
    acc_out = take() if steps else None
    if n_send:
        send_v, send_sem, sendo_sem = take(3)
    if steps:
        hid_v, d_v, acc_v, hid_sem, d_sem, acc_sem, acco_sem = take(7)
    place = info[0]
    part_rows = gate.shape[0] // across
    waits, copies, sends = [], [], []
    if steps:
        acc_in, acc_out = acc_in[0], acc_out[0]
        half = acc_in.shape[0] // 2
        for n in range(steps):
            waits.append(begin(hids[n], hid_v.at[n], hid_sem.at[n]))
            for s in range(2):
                own = info[1] * part_rows + info[2 + 4 * n + s]
                waits.append(
                    begin(rows_at(down, own, width), d_v.at[n, s, 0], d_sem.at[n, s, 0])
                )
                for j in range(1, across):
                    dst, sem = d_v.at[n, s, j], d_sem.at[n, s, j]
                    for i in range(deep):
                        here = i if s == 0 else deep - 1 - i

                        @pl.when(place == here)
                        def _(src=got[n][i][j - 1], dst=dst, sem=sem):
                            pltpu.make_async_copy(
                                src.at[pl.ds(2 * width, width)], dst, sem
                            ).start()

                    waits.append(
                        pltpu.make_async_copy(
                            got[n][0][j - 1].at[pl.ds(2 * width, width)], dst, sem
                        )
                    )
        tile = half // 2
        acc_copies = [
            begin(
                acc_in.at[pl.ds(i * tile, tile)],
                acc_v.at[pl.ds(i * tile, tile)],
                acc_sem.at[i],
            )
            for i in range(4)
        ]
    base = 2 + 4 * steps
    for j in range(n_send):
        for k, ref in enumerate((gate, up, down)):
            sends.append(
                begin(
                    rows_at(ref, info[base + j], width),
                    send_v.at[j, pl.ds(k * width, width)],
                    send_sem.at[j, k],
                )
            )
    for copy in sends:
        copy.wait()
    for j in range(n_send):
        copies.append(begin(send_v.at[j], sent[j], sendo_sem.at[j]))
    if steps:
        for copy in waits:
            copy.wait()
        feat = d_v.shape[-1]
        for i in range(4):
            s = i // 2
            here = pl.ds(i * tile, tile)
            acc_copies[i].wait()
            for j in range(across):
                total = acc_v[here, pl.ds(j * feat, feat)]
                for n in range(steps):
                    hidden = hid_v[n, here, :]
                    valid = info[4 + 4 * n + s] > 0
                    hidden = jnp.where(valid, hidden, jnp.zeros_like(hidden))
                    total += lax.dot_general(
                        hidden,
                        d_v[n, s, j],
                        (((1,), (0,)), ((), ())),
                        preferred_element_type=jnp.float32,
                    )
                acc_v[here, pl.ds(j * feat, feat)] = total
            copies.append(begin(acc_v.at[here], acc_out.at[here], acco_sem.at[i]))
    for copy in copies:
        copy.wait()


def call(kernel, args, outs, scratch, aliases, flops, nbytes, name):
    return list(
        pl.pallas_call(
            kernel,
            out_shape=outs,
            in_specs=[pl.BlockSpec(memory_space=pltpu.SMEM)]
            + [pl.BlockSpec(memory_space=pl.ANY)] * (len(args) - 1),
            out_specs=[pl.BlockSpec(memory_space=pl.ANY)] * len(outs),
            scratch_shapes=scratch,
            input_output_aliases=aliases,
            compiler_params=pltpu.CompilerParams(vmem_limit_bytes=VMEM),
            cost_estimate=pl.CostEstimate(
                flops=flops, bytes_accessed=nbytes, transcendentals=0
            ),
            name=name,
        )(*args)
    )


def body(tokens, routes, combine, gate_weight, up_weight, down_weight):
    hop, width, ahead, batch = HOP, WIDTH, AHEAD, BATCH
    expert = lax.axis_index("member")
    members = lax.axis_size("member")
    groups = lax.axis_size("fsdp")
    me = lax.axis_index("fsdp")
    deep, across = grid_of(groups)
    z, x = me // across, lax.rem(me, across)
    tok_rows = tokens.shape[0]
    capacity = 3 * tok_rows // members
    gate_weight, up_weight, down_weight = gate_weight[0], up_weight[0], down_weight[0]
    hidden_all, feat = gate_weight.shape
    part_rows = hidden_all // across
    n_chunks = -(-part_rows // width)
    total_rows = capacity * groups
    half_rows = total_rows // 2
    bf, f32 = jnp.bfloat16, jnp.float32
    dma = pltpu.SemaphoreType.DMA

    def swap(array, dz, dx):
        perm = [
            (a * across + b, (a ^ dz) * across + (b ^ dx))
            for a in range(deep)
            for b in range(across)
        ]
        return lax.ppermute(array, "fsdp", perm)

    def pairing(array, slot):
        perm = []
        for m in range(members):
            for a in range(deep):
                b = a ^ 1 if slot == 0 else ((a + 1) ^ 1) - 1
                for c in range(across):
                    there = (m, b) if 0 <= b < deep else (m ^ 1, a)
                    perm.append(
                        (m * groups + a * across + c, there[0] * groups + there[1] * across + c)
                    )
        return lax.ppermute(array, ("member", "fsdp"), perm)

    def start_of(chunk):
        return jnp.minimum(jnp.clip(chunk, 0, n_chunks - 1) * width, part_rows - width)

    got = {}

    def hand_over(k, arrays):
        got[k] = [swap(a, 0, j + 1) for j, a in enumerate(arrays)]

    def send_start(k, j):
        return (x ^ j) * part_rows + min(k * width, part_rows - width)

    def hand_over_early(k, weights):
        hand_over(
            k,
            [
                jnp.concatenate(
                    [lax.dynamic_slice_in_dim(w, send_start(k, j), width, 0) for w in weights]
                )
                for j in range(1, across)
            ],
        )

    weights = (gate_weight, up_weight, down_weight)
    early = min(ahead, n_chunks)
    for k in range(min(2, early)):
        hand_over_early(k, weights)

    picked = routes == expert
    chosen = jnp.any(picked, axis=1)
    token_weight = jnp.sum(jnp.where(picked, combine, jnp.zeros_like(combine)), axis=1)
    position = jnp.cumsum(chosen.astype(jnp.int32)) - 1
    slot_ids = jnp.arange(capacity, dtype=jnp.int32)
    placed = (position[:, None] == slot_ids[None, :]) & chosen[:, None]
    packed = lax.dot_general(
        placed.astype(bf), tokens, (((0,), (0,)), ((), ())), preferred_element_type=f32
    ).astype(bf)
    token_ids = jnp.arange(tok_rows, dtype=jnp.int32)
    came_from = jnp.sum(jnp.where(placed, token_ids[:, None] + 1, 0), axis=0)
    weight = jnp.sum(jnp.where(placed, token_weight[:, None], 0.0), axis=0)
    high = lax.reduce_precision(weight, 8, 7)
    middle = lax.reduce_precision(weight - high, 8, 7)
    low = weight - high - middle
    notes = jnp.stack(
        [(came_from // 128).astype(f32), (came_from % 128).astype(f32), high, middle, low], axis=1
    ).astype(bf)
    notes = jnp.pad(notes, ((0, 0), (0, 128 - notes.shape[1])))

    def pick(array, index):
        return lax.dynamic_index_in_dim(array, index, 0, keepdims=False)

    def columns(array, index, size):
        return lax.dynamic_slice_in_dim(array, index * size, size, 1)

    pieces = []
    for k in range(deep):
        piece = jnp.concatenate([columns(packed, z ^ k, across * feat), notes], axis=1)
        pieces.append(swap(piece, k, 0) if k else piece)
    pieces = jnp.stack(pieces)
    mine = jnp.concatenate([pick(pieces, z ^ a) for a in range(deep)])
    mine, got[0] = lax.optimization_barrier((mine, got[0]))
    by_group = [swap(mine, 0, i) if i else mine for i in range(across)]
    by_group, weights = lax.optimization_barrier((by_group, weights))
    for k in range(2, early):
        hand_over_early(k, weights)
    toks = jnp.stack(
        [jnp.concatenate([columns(g, x ^ j, feat) for g in by_group]) for j in range(across)]
    )
    notes = jnp.concatenate([g[:, across * feat :] for g in by_group])[:, :5].astype(f32)
    notes = notes.T.reshape(5, across * deep, capacity)
    came_from = (notes[0] * 128.0 + notes[1]).astype(jnp.int32) - 1
    weight = notes[2] + notes[3] + notes[4]

    reach = hop * (deep - 1)
    n_steps = n_chunks + 2 * reach
    acc = jnp.zeros((total_rows, across * feat), f32)
    msgs, waiting, order = {}, [], None
    early_at = reach + n_chunks - 1 + hop * (deep // 2 - 1)
    early_half = jnp.where(z < deep // 2, 0, 1)

    def own_parts(which):
        rows = lax.dynamic_slice_in_dim(acc, which * half_rows, half_rows, 0)
        return [
            swap(rows[:, j * feat : (j + 1) * feat].astype(bf), 0, j) for j in range(1, across)
        ]

    last_skip = n_chunks * width - part_rows

    def candidates(base):
        return [a for i in range(deep) for a in got[min(max(base - hop * i, 0), n_chunks - 1)]]

    for t in range(n_steps):
        sums = t < n_chunks + reach
        back = t >= reach
        before = t - hop
        sums_in = sums and before >= 0
        back_in = back and before >= reach
        cfg = (deep, across, width, sums, sums_in, back, back_in)
        skip = last_skip if t - reach == n_chunks - 1 else 0
        up_c, dn_c = t - hop * z, t - hop * (deep - 1 - z)
        info = jnp.stack([z, x, start_of(up_c), start_of(dn_c), jnp.int32(skip)]).astype(
            jnp.int32
        )
        if order is not None:
            info, order = lax.optimization_barrier((info, order))
            if "acc" in order:
                acc = order["acc"]
            if "sent" in order:
                hand_over(t - 1 + early, order["sent"])
            order = None
        if t == early_at + 3:
            info, early_parts = lax.optimization_barrier((info, early_parts))
        args, outs, scratch = [info], [], []
        if sums:
            args += [gate_weight, up_weight, toks] + candidates(t)
            scratch += [
                pltpu.VMEM((across, total_rows, feat), bf),
                pltpu.VMEM((2, across, 2 * width, feat), bf),
                dma((2,)),
                dma((2, across, 2)),
            ]
        if sums_in or back_in:
            args += list(msgs[before])
            scratch += [pltpu.VMEM((2,) + msgs[before][0].shape, bf), dma((2,))]
        out_width = 2 * width * sums + width * back
        outs += [jax.ShapeDtypeStruct((half_rows, out_width), bf)] * 2
        scratch += [pltpu.VMEM((2, half_rows, out_width), bf), dma((2,))]
        if back:
            outs += [jax.ShapeDtypeStruct((total_rows, width), bf)]
            scratch += [pltpu.VMEM((total_rows, width), bf), dma]
        res = call(
            functools.partial(chain_kernel, cfg),
            args,
            outs,
            scratch,
            {},
            4 * total_rows * width * across * feat * sums,
            8 * 1024 * 1024,
            "chain_step",
        )
        if back:
            waiting.append((t, res[2]))

        next_k = t + early
        n_send = across - 1 if next_k < n_chunks else 0
        flush = len(waiting) == batch or t in (early_at, n_steps - 1)
        steps = len(waiting) if flush else 0
        if not steps and not n_send:
            if t + hop < n_steps:
                msgs[t] = (pairing(res[0], 0), pairing(res[1], 1))
            continue
        done, entries = [], [z, x]
        if steps:
            done, waiting = waiting, []
        for at, _ in done:
            up_c, dn_c = at - reach - hop * z, at - reach - hop * (deep - 1 - z)
            entries += [start_of(up_c), start_of(dn_c)]
            entries += [((c >= 0) & (c < n_chunks)).astype(jnp.int32) for c in (up_c, dn_c)]
        entries += [send_start(next_k, j + 1) for j in range(n_send)]
        side_info = jnp.stack([jnp.int32(e) for e in entries]).astype(jnp.int32)
        side_info, res = lax.optimization_barrier((side_info, res))
        if t + hop < n_steps:
            msgs[t] = (pairing(res[0], 0), pairing(res[1], 1))
        args = [side_info]
        args += [gate_weight, up_weight, down_weight] + [hid for _, hid in done]
        for at, _ in done:
            args += candidates(at - reach)
        aliases, outs, scratch = {}, [], []
        outs += [jax.ShapeDtypeStruct((3 * width, feat), bf)] * n_send
        if n_send:
            scratch += [
                pltpu.VMEM((n_send, 3 * width, feat), bf),
                dma((n_send, 3)),
                dma((n_send,)),
            ]
        if steps:
            aliases = {len(args): n_send}
            args += [acc]
            outs += [jax.ShapeDtypeStruct(acc.shape, f32)]
            scratch += [
                pltpu.VMEM((steps, total_rows, width), bf),
                pltpu.VMEM((steps, 2, across, width, feat), bf),
                pltpu.VMEM(acc.shape, f32),
                dma((steps,)),
                dma((steps, 2, across)),
                dma((4,)),
                dma((4,)),
            ]
        res = call(
            functools.partial(side_kernel, (deep, across, width, steps, n_send)),
            args,
            outs,
            scratch,
            aliases,
            2 * total_rows * width * across * feat * steps,
            (12 if steps else 2) * 1024 * 1024,
            "side_step",
        )
        order = {}
        if steps:
            order["acc"] = acc = res.pop()
        if n_send:
            order["sent"] = res
        if t == early_at:
            early_parts = own_parts(early_half)

    late_parts = own_parts(1 - early_half)
    group_rows = total_rows // across
    whole = acc[:, :feat]
    for j in range(1, across):
        first, second = early_parts[j - 1], late_parts[j - 1]
        part = jnp.concatenate(
            [
                jnp.where(early_half == 0, first, second),
                jnp.where(early_half == 0, second, first),
            ]
        )
        part = jnp.concatenate(
            [part[(i ^ j) * group_rows : ((i ^ j) + 1) * group_rows] for i in range(across)]
        )
        whole = whole + part.astype(f32)
    whole = whole.reshape(across * deep, capacity, feat)
    spread = jnp.where(
        came_from[:, None, :] == token_ids[None, :, None], weight[:, None, :], 0.0
    )
    weighted = lax.dot_general(
        spread,
        whole,
        (((2,), (1,)), ((0,), (0,))),
        precision=lax.Precision.HIGHEST,
        preferred_element_type=f32,
    ).reshape(across, deep, tok_rows, feat)
    weighted = jnp.stack([pick(weighted, x ^ b) for b in range(across)], axis=1)
    share = groups // members
    left = weighted.reshape(members, share * tok_rows, feat)
    bit = 1
    while bit < members:
        pairs = left.reshape(left.shape[0] // 2, 2, share * tok_rows, feat)
        side = (expert // bit) % 2
        keep, give = (
            lax.dynamic_index_in_dim(pairs, s, 1, keepdims=False) for s in (side, 1 - side)
        )
        give = give if bit == 1 else give.astype(bf)
        came = lax.ppermute(give, "member", [(m, m ^ bit) for m in range(members)])
        left = keep + came.astype(f32)
        bit *= 2
    mixed = left.astype(bf).reshape(share, tok_rows, feat)
    slot = lax.rem(me, share)
    parts = []
    for j in range(share):
        perm = []
        for r in range(members):
            for f in range(groups):
                block = r * share + ((f % share) ^ j)
                perm.append((r * groups + f, (f // share) * groups + block))
        parts.append(lax.ppermute(pick(mixed, slot ^ j), ("member", "fsdp"), perm))
    parts = jnp.stack(parts)
    return jnp.concatenate([pick(parts, slot ^ c) for c in range(share)], axis=1)


def solution(mesh):
    placed = (
        P("fsdp", None),
        P("fsdp", None),
        P("fsdp", None),
        P("member", None, "fsdp"),
        P("member", None, "fsdp"),
        P("member", None, "fsdp"),
    )
    return jax.shard_map(
        body, mesh=mesh, in_specs=placed, out_specs=P("fsdp", "member"), check_vma=False
    )
```

```python
import functools

import jax
import jax.numpy as jnp
from jax import lax
from jax.experimental import pallas as pl
from jax.experimental.pallas import tpu as pltpu
from jax.sharding import PartitionSpec as P

WIDTH = 256
HOP = 2
AHEAD = 3
BATCH = 2
VMEM = 62 * 1024 * 1024


def grid_of(size):
    across = 1
    while across * across * 4 <= size:
        across *= 2
    return size // across, across


def begin(src, dst, sem):
    copy = pltpu.make_async_copy(src, dst, sem)
    copy.start()
    return copy


def taker(refs):
    refs = list(refs)

    def take(count=1):
        out = refs[:count]
        del refs[:count]
        return out

    return take


def rows_at(ref, start, width):
    return ref.at[pl.ds(pl.multiple_of(start, 16), width)]


def chain_kernel(cfg, *refs):
    deep, across, width, sums, sums_in, sums_out, back, back_in = cfg
    take = taker(refs)
    (info,) = take()
    if sums:
        gate, up, toks = take(3)
        got = [take(across - 1) for _ in range(deep)]
    came = take(2) if sums_in or back_in else None
    sent = take(2)
    (hid_out,) = take() if back else (None,)
    if sums:
        toks_v, w_v, tok_sem, w_sem = take(4)
    if came:
        came_v, came_sem = take(2)
    sent_v, sent_sem = take(2)
    if back:
        hid_v, hid_sem = take(2)
    place = info[0]
    odd = lax.rem(place, 2)
    wide = 2 * width if sums_out else 0
    in_wide = came[0].shape[1] - (width if back_in else 0) if came else 0
    half = sent[0].shape[0]
    copies = []

    waits = [[], []]
    for s in range(2):
        if came:
            for slot in range(2):

                @pl.when(lax.rem(odd + s, 2) == 1 - slot)
                def _(src=came[slot], s=s):
                    pltpu.make_async_copy(src, came_v.at[s], came_sem.at[s]).start()

            waits[s].append(pltpu.make_async_copy(came[0], came_v.at[s], came_sem.at[s]))
    if sums:
        part_rows = gate.shape[0] // across
        tok_copies = [
            begin(
                toks.at[:, pl.ds(s * half, half)],
                toks_v.at[:, pl.ds(s * half, half)],
                tok_sem.at[s],
            )
            for s in (1, 0)
        ][::-1]
        for s in range(2):
            own = info[1] * part_rows + info[2 + s]
            for k, ref in enumerate((gate, up)):
                waits[s].append(
                    begin(
                        rows_at(ref, own, width),
                        w_v.at[s, 0, pl.ds(k * width, width)],
                        w_sem.at[s, 0, k],
                    )
                )
            for j in range(1, across):
                dst, sem = w_v.at[s, j], w_sem.at[s, j, 0]
                for i in range(deep):
                    here = i if s == 0 else deep - 1 - i

                    @pl.when(place == here)
                    def _(src=got[i][j - 1], dst=dst, sem=sem):
                        pltpu.make_async_copy(src.at[pl.ds(0, 2 * width)], dst, sem).start()

                waits[s].append(
                    pltpu.make_async_copy(got[0][j - 1].at[pl.ds(0, 2 * width)], dst, sem)
                )

    ends = []
    for s in range(2):
        for copy in waits[s]:
            copy.wait()
        if not sums:
            continue
        mine = 1 - s
        tok_copies[mine].wait()
        total = None
        for j in range(across):
            term = lax.dot_general(
                toks_v[j, pl.ds(mine * half, half), :],
                w_v[s, j],
                (((1,), (1,)), ((), ())),
                preferred_element_type=jnp.float32,
            )
            total = term if total is None else total + term
        if sums_in:
            first = place == (0 if s == 0 else deep - 1)
            before = came_v[s, :, : 2 * width].astype(jnp.float32)
            total = total + jnp.where(first, 0.0, before)
        if sums_out:
            sent_v[s, :, : 2 * width] = total.astype(jnp.bfloat16)
        if back:
            value, upper = total[:, :width], total[:, width:]
            hidden = value / (1.0 + jnp.exp(-value)) * upper
            column = lax.broadcasted_iota(jnp.int32, hidden.shape, 1)
            ends.append(jnp.where(column >= info[4], hidden, 0.0).astype(jnp.bfloat16))
    if back:
        for s in range(2):
            value = came_v[s, :, in_wide:] if back_in else None
            if sums:
                at_end = place == (0 if s == 0 else deep - 1)
                other = value if back_in else jnp.zeros_like(ends[1 - s])
                value = jnp.where(at_end, ends[1 - s], other)
            sent_v[s, :, wide:] = value
            hid_v[pl.ds(s * half, half)] = value
    for s in range(2):
        for slot in range(2):

            @pl.when(lax.rem(odd + s, 2) == slot)
            def _(dst=sent[slot], s=s):
                pltpu.make_async_copy(sent_v.at[s], dst, sent_sem.at[s]).start()

        copies.append(pltpu.make_async_copy(sent_v.at[s], sent[0], sent_sem.at[s]))
    if back:
        copies.append(begin(hid_v, hid_out, hid_sem))
    for copy in copies:
        copy.wait()


def side_kernel(cfg, *refs):
    deep, across, width, steps_direct, offsets, n_send, kinds = cfg
    steps = len(steps_direct)
    take = taker(refs)
    (info,) = take()
    gate, up, down = take(3)
    hids = [take(2) if direct else take() for direct in steps_direct]
    got = [[take(across - 1) for _ in range(deep)] for _ in range(steps)]
    acc_in = take() if steps else None
    sent = take(n_send)
    acc_out = take() if steps else None
    if n_send:
        send_v, send_sem, sendo_sem = take(3)
    if steps:
        hid_v, d_v, acc_v, hid_sem, d_sem, acc_sem, acco_sem = take(7)
    place = info[0]
    part_rows = gate.shape[0] // across
    waits, copies, sends = [], [], []
    if steps:
        acc_in, acc_out = acc_in[0], acc_out[0]
        half = acc_in.shape[0] // 2
        for n in range(steps):
            for s in range(2):
                here = hid_v.at[n, pl.ds(s * half, half)]
                sem = hid_sem.at[n, s]
                if len(hids[n]) == 1:
                    waits.append(begin(hids[n][0].at[pl.ds(s * half, half)], here, sem))
                    continue
                for slot in range(2):

                    @pl.when(lax.rem(place + s, 2) == 1 - slot)
                    def _(src=hids[n][slot], here=here, sem=sem):
                        pltpu.make_async_copy(src, here, sem).start()

                waits.append(pltpu.make_async_copy(hids[n][0], here, sem))
            for s in range(2):
                own = info[1] * part_rows + info[2 + 4 * n + s]
                waits.append(
                    begin(rows_at(down, own, width), d_v.at[n, s, 0], d_sem.at[n, s, 0])
                )
                for j in range(1, across):
                    dst, sem = d_v.at[n, s, j], d_sem.at[n, s, j]
                    for i in range(deep):
                        here = i if s == 0 else deep - 1 - i

                        @pl.when(place == here)
                        def _(src=got[n][i][j - 1], at=offsets[n][i], dst=dst, sem=sem):
                            pltpu.make_async_copy(src.at[pl.ds(at, width)], dst, sem).start()

                    src = got[n][0][j - 1].at[pl.ds(offsets[n][0], width)]
                    waits.append(pltpu.make_async_copy(src, dst, sem))
        tile = half // 2
        acc_loads = [
            pltpu.make_async_copy(
                acc_in.at[pl.ds(i * tile, tile)], acc_v.at[pl.ds(i * tile, tile)], acc_sem.at[i]
            )
            for i in range(4)
        ]
        acc_stores = [
            pltpu.make_async_copy(
                acc_v.at[pl.ds(i * tile, tile)], acc_out.at[pl.ds(i * tile, tile)], acco_sem.at[i]
            )
            for i in range(4)
        ]
        needed = []
        for s in range(2):
            flags = [info[4 + 4 * n + s] for n in range(steps)]
            needed.append(functools.reduce(jnp.maximum, flags) > 0)

            @pl.when(needed[s])
            def _(s=s):
                for i in (2 * s, 2 * s + 1):
                    acc_loads[i].start()

    base = 2 + 4 * steps
    for j in range(n_send):
        for k, kind in enumerate(kinds):
            ref = (gate, up, down)[kind]
            sends.append(
                begin(
                    rows_at(ref, info[base + 2 * j + kind // 2], width),
                    send_v.at[j, pl.ds(k * width, width)],
                    send_sem.at[j, k],
                )
            )
    for copy in sends:
        copy.wait()
    for j in range(n_send):
        copies.append(begin(send_v.at[j], sent[j], sendo_sem.at[j]))
    if steps:
        for copy in waits:
            copy.wait()
        feat = d_v.shape[-1]
        for s in range(2):

            @pl.when(needed[s])
            def _(s=s):
                for i in (2 * s, 2 * s + 1):
                    here = pl.ds(i * tile, tile)
                    acc_loads[i].wait()
                    for j in range(across):
                        total = acc_v[here, pl.ds(j * feat, feat)]
                        for n in range(steps):
                            hidden = hid_v[n, here, :]
                            valid = info[4 + 4 * n + s] > 0
                            hidden = jnp.where(valid, hidden, jnp.zeros_like(hidden))
                            total += lax.dot_general(
                                hidden,
                                d_v[n, s, j],
                                (((1,), (0,)), ((), ())),
                                preferred_element_type=jnp.float32,
                            )
                        acc_v[here, pl.ds(j * feat, feat)] = total
                    acc_stores[i].start()

        for s in range(2):

            @pl.when(needed[s])
            def _(s=s):
                for i in (2 * s, 2 * s + 1):
                    acc_stores[i].wait()

    for copy in copies:
        copy.wait()


def call(kernel, args, outs, scratch, aliases, flops, nbytes, name):
    return list(
        pl.pallas_call(
            kernel,
            out_shape=outs,
            in_specs=[pl.BlockSpec(memory_space=pltpu.SMEM)]
            + [pl.BlockSpec(memory_space=pl.ANY)] * (len(args) - 1),
            out_specs=[pl.BlockSpec(memory_space=pl.ANY)] * len(outs),
            scratch_shapes=scratch,
            input_output_aliases=aliases,
            compiler_params=pltpu.CompilerParams(vmem_limit_bytes=VMEM),
            cost_estimate=pl.CostEstimate(
                flops=flops, bytes_accessed=nbytes, transcendentals=0
            ),
            name=name,
        )(*args)
    )


def body(tokens, routes, combine, gate_weight, up_weight, down_weight):
    hop, width, ahead, batch = HOP, WIDTH, AHEAD, BATCH
    expert = lax.axis_index("member")
    members = lax.axis_size("member")
    groups = lax.axis_size("fsdp")
    me = lax.axis_index("fsdp")
    deep, across = grid_of(groups)
    z, x = me // across, lax.rem(me, across)
    tok_rows = tokens.shape[0]
    capacity = 3 * tok_rows // members
    gate_weight, up_weight, down_weight = gate_weight[0], up_weight[0], down_weight[0]
    hidden_all, feat = gate_weight.shape
    part_rows = hidden_all // across
    n_chunks = -(-part_rows // width)
    total_rows = capacity * groups
    half_rows = total_rows // 2
    bf, f32 = jnp.bfloat16, jnp.float32
    dma = pltpu.SemaphoreType.DMA

    def swap(array, dz, dx):
        perm = [
            (a * across + b, (a ^ dz) * across + (b ^ dx))
            for a in range(deep)
            for b in range(across)
        ]
        return lax.ppermute(array, "fsdp", perm)

    def pairing(array, slot):
        perm = []
        for m in range(members):
            for a in range(deep):
                b = a ^ 1 if slot == 0 else ((a + 1) ^ 1) - 1
                for c in range(across):
                    there = (m, b) if 0 <= b < deep else (m ^ 1, a)
                    perm.append(
                        (m * groups + a * across + c, there[0] * groups + there[1] * across + c)
                    )
        return lax.ppermute(array, ("member", "fsdp"), perm)

    def start_of(chunk):
        return jnp.minimum(jnp.clip(chunk, 0, n_chunks - 1) * width, part_rows - width)

    got = {}

    def hand_over(k, arrays):
        got[k] = [swap(a, 0, j + 1) for j, a in enumerate(arrays)]

    def send_start(k, j):
        return (x ^ j) * part_rows + min(k * width, part_rows - width)

    reach = hop * (deep - 1)

    def kinds_of(k):
        return (0, 1) * (k < n_chunks) + (2,) * (reach <= k < n_chunks + reach)

    def send_starts(k):
        return [send_start(c, j) for j in range(1, across) for c in (k, max(k - reach, 0))]

    def message(k):
        return [jax.ShapeDtypeStruct((len(kinds_of(k)) * width, feat), bf)] * (across - 1)

    def lay_out(k, weights):
        n_send, rows = across - 1, len(kinds_of(k)) * width
        return call(
            functools.partial(side_kernel, (deep, across, width, (), (), n_send, kinds_of(k))),
            [jnp.stack([z, x] + send_starts(k)).astype(jnp.int32)] + list(weights),
            message(k),
            [pltpu.VMEM((n_send, rows, feat), bf), dma((n_send, 3)), dma((n_send,))],
            {},
            0,
            2 * 1024 * 1024,
            "side_step",
        )

    weights = (gate_weight, up_weight, down_weight)
    early = min(ahead, n_chunks)
    firsts = [lay_out(k, weights) for k in range(early)]
    firsts[0], tokens = lax.optimization_barrier((firsts[0], tokens))
    hand_over(0, firsts[0])

    picked = routes == expert
    chosen = jnp.any(picked, axis=1)
    token_weight = jnp.sum(jnp.where(picked, combine, jnp.zeros_like(combine)), axis=1)
    position = jnp.cumsum(chosen.astype(jnp.int32)) - 1
    slot_ids = jnp.arange(capacity, dtype=jnp.int32)
    placed = (position[:, None] == slot_ids[None, :]) & chosen[:, None]
    packed = lax.dot_general(
        placed.astype(bf), tokens, (((0,), (0,)), ((), ())), preferred_element_type=f32
    ).astype(bf)
    token_ids = jnp.arange(tok_rows, dtype=jnp.int32)
    came_from = jnp.sum(jnp.where(placed, token_ids[:, None] + 1, 0), axis=0)
    weight = jnp.sum(jnp.where(placed, token_weight[:, None], 0.0), axis=0)
    high = lax.reduce_precision(weight, 8, 7)
    middle = lax.reduce_precision(weight - high, 8, 7)
    low = weight - high - middle
    notes = jnp.stack(
        [(came_from // 128).astype(f32), (came_from % 128).astype(f32), high, middle, low], axis=1
    ).astype(bf)
    notes = jnp.pad(notes, ((0, 0), (0, 128 - notes.shape[1])))

    def pick(array, index):
        return lax.dynamic_index_in_dim(array, index, 0, keepdims=False)

    def columns(array, index, size):
        return lax.dynamic_slice_in_dim(array, index * size, size, 1)

    pieces = []
    for k in range(deep):
        piece = jnp.concatenate([columns(packed, z ^ k, across * feat), notes], axis=1)
        pieces.append(swap(piece, k, 0) if k else piece)
    pieces = jnp.stack(pieces)
    mine = jnp.concatenate([pick(pieces, z ^ a) for a in range(deep)])
    mine, got[0] = lax.optimization_barrier((mine, got[0]))
    by_group = [swap(mine, 0, i) if i else mine for i in range(across)]
    by_group, firsts = lax.optimization_barrier((by_group, firsts))
    for k in range(1, early):
        hand_over(k, firsts[k])
    toks = jnp.stack(
        [jnp.concatenate([columns(g, x ^ j, feat) for g in by_group]) for j in range(across)]
    )
    notes = jnp.concatenate([g[:, across * feat :] for g in by_group])[:, :5].astype(f32)
    notes = notes.T.reshape(5, across * deep, capacity)
    came_from = (notes[0] * 128.0 + notes[1]).astype(jnp.int32) - 1
    weight = notes[2] + notes[3] + notes[4]

    n_steps = n_chunks + 2 * reach
    acc = jnp.zeros((total_rows, across * feat), f32)
    msgs, waiting, order = {}, [], None
    early_at = reach + n_chunks - 1 + hop * (deep // 2 - 1)
    early_half = jnp.where(z < deep // 2, 0, 1)

    def own_parts(which):
        rows = lax.dynamic_slice_in_dim(acc, which * half_rows, half_rows, 0)
        return [
            swap(rows[:, j * feat : (j + 1) * feat].astype(bf), 0, j) for j in range(1, across)
        ]

    last_skip = n_chunks * width - part_rows

    def send_on(t, res):
        if t == n_chunks + reach - 1:
            msgs[t - 1], res = lax.optimization_barrier((msgs[t - 1], res))
        msgs[t] = (pairing(res[0], 0), pairing(res[1], 1))
        if t == n_chunks + reach - 1:
            for u in range(t + 1, n_steps - hop):
                msgs[u] = (pairing(msgs[u - hop][1], 0), pairing(msgs[u - hop][0], 1))

    def chunks(base):
        return [min(max(base - hop * i, 0), n_chunks - 1) for i in range(deep)]

    for t in range(n_steps):
        sums = t < n_chunks + reach
        back = t >= reach
        if not sums:
            waiting.append((t, msgs[t - hop]))
        if sums:
            before = t - hop
            sums_in = sums and before >= 0
            sums_out = t + hop < n_chunks + reach
            back_in = back and before >= reach
            cfg = (deep, across, width, sums, sums_in, sums_out, back, back_in)
            skip = last_skip if t - reach == n_chunks - 1 else 0
            up_c, dn_c = t - hop * z, t - hop * (deep - 1 - z)
            info = jnp.stack([z, x, start_of(up_c), start_of(dn_c), jnp.int32(skip)]).astype(
                jnp.int32
            )
            if order is not None:
                info, order = lax.optimization_barrier((info, order))
                if "acc" in order:
                    acc = order["acc"]
                if "sent" in order:
                    hand_over(t - 1 + early, order["sent"])
                order = None
            args, outs, scratch = [info], [], []
            if sums:
                args += [gate_weight, up_weight, toks] + [a for c in chunks(t) for a in got[c]]
                scratch += [
                    pltpu.VMEM((across, total_rows, feat), bf),
                    pltpu.VMEM((2, across, 2 * width, feat), bf),
                    dma((2,)),
                    dma((2, across, 2)),
                ]
            if sums_in or back_in:
                args += list(msgs[before])
                scratch += [pltpu.VMEM((2,) + msgs[before][0].shape, bf), dma((2,))]
            out_width = 2 * width * sums_out + width * back
            outs += [jax.ShapeDtypeStruct((half_rows, out_width), bf)] * 2
            scratch += [pltpu.VMEM((2, half_rows, out_width), bf), dma((2,))]
            if back:
                outs += [jax.ShapeDtypeStruct((total_rows, width), bf)]
                scratch += [pltpu.VMEM((total_rows, width), bf), dma]
            res = call(
                functools.partial(chain_kernel, cfg),
                args,
                outs,
                scratch,
                {},
                4 * total_rows * width * across * feat * sums,
                8 * 1024 * 1024,
                "chain_step",
            )
            if back:
                waiting.append((t, [res[2]]))

        next_k = t + early
        kinds = kinds_of(next_k)
        n_send = across - 1 if kinds else 0
        flush = (len(waiting) == batch and t < early_at) or t in (early_at, n_steps - 1)
        steps = len(waiting) if flush else 0
        if not steps and not n_send:
            if sums:
                send_on(t, res)
            continue
        done, entries = [], [z, x]
        if steps:
            done, waiting = waiting, []
        for at, _ in done:
            up_c, dn_c = at - reach - hop * z, at - reach - hop * (deep - 1 - z)
            entries += [start_of(up_c), start_of(dn_c)]
            entries += [((c >= 0) & (c < n_chunks)).astype(jnp.int32) for c in (up_c, dn_c)]
        if n_send:
            entries += send_starts(next_k)
        side_info = jnp.stack([jnp.int32(e) for e in entries]).astype(jnp.int32)
        if t == n_steps - 1:
            side_info, early_parts = lax.optimization_barrier((side_info, early_parts))
        if sums:
            side_info, res = lax.optimization_barrier((side_info, res))
            send_on(t, res)
        if t >= n_chunks + reach - 1 and t + 1 in msgs:
            side_info, msgs[t + 1] = lax.optimization_barrier((side_info, msgs[t + 1]))
        args = [side_info]
        args += [gate_weight, up_weight, down_weight] + [h for _, hid in done for h in hid]
        offsets = []
        for at, _ in done:
            args += [a for c in chunks(at - reach) for a in got[c + reach]]
            offsets.append(
                tuple(2 * width * (c + reach < n_chunks) for c in chunks(at - reach))
            )
        aliases, outs, scratch = {}, [], []
        if n_send:
            outs += message(next_k)
            scratch += [
                pltpu.VMEM((n_send, len(kinds) * width, feat), bf),
                dma((n_send, 3)),
                dma((n_send,)),
            ]
        if steps:
            aliases = {len(args): n_send}
            args += [acc]
            outs += [jax.ShapeDtypeStruct(acc.shape, f32)]
            scratch += [
                pltpu.VMEM((steps, total_rows, width), bf),
                pltpu.VMEM((steps, 2, across, width, feat), bf),
                pltpu.VMEM(acc.shape, f32),
                dma((steps, 2)),
                dma((steps, 2, across)),
                dma((4,)),
                dma((4,)),
            ]
        res = call(
            functools.partial(
                side_kernel,
                (
                    deep,
                    across,
                    width,
                    tuple(len(h) == 2 for _, h in done),
                    tuple(offsets),
                    n_send,
                    kinds,
                ),
            ),
            args,
            outs,
            scratch,
            aliases,
            2 * total_rows * width * across * feat * steps,
            (12 if steps else 2) * 1024 * 1024,
            "side_step",
        )
        order = {}
        if steps:
            order["acc"] = acc = res.pop()
        if n_send:
            order["sent"] = res
        if t == early_at:
            early_parts = own_parts(early_half)

    late_parts = own_parts(1 - early_half)
    group_rows = total_rows // across
    whole = acc[:, :feat]
    for j in range(1, across):
        first, second = early_parts[j - 1], late_parts[j - 1]
        part = jnp.concatenate(
            [
                jnp.where(early_half == 0, first, second),
                jnp.where(early_half == 0, second, first),
            ]
        )
        part = jnp.concatenate(
            [part[(i ^ j) * group_rows : ((i ^ j) + 1) * group_rows] for i in range(across)]
        )
        whole = whole + part.astype(f32)
    whole = whole.reshape(across * deep, capacity, feat)
    spread = jnp.where(
        came_from[:, None, :] == token_ids[None, :, None], weight[:, None, :], 0.0
    )
    weighted = lax.dot_general(
        spread,
        whole,
        (((2,), (1,)), ((0,), (0,))),
        precision=lax.Precision.HIGHEST,
        preferred_element_type=f32,
    ).reshape(across, deep, tok_rows, feat)
    weighted = jnp.stack([pick(weighted, x ^ b) for b in range(across)], axis=1)
    share = groups // members
    left = weighted.reshape(members, share * tok_rows, feat)
    bit = 1
    while bit < members:
        pairs = left.reshape(left.shape[0] // 2, 2, share * tok_rows, feat)
        side = (expert // bit) % 2
        keep, give = (
            lax.dynamic_index_in_dim(pairs, s, 1, keepdims=False) for s in (side, 1 - side)
        )
        give = give if bit == 1 else give.astype(bf)
        came = lax.ppermute(give, "member", [(m, m ^ bit) for m in range(members)])
        left = keep + came.astype(f32)
        bit *= 2
    mixed = left.astype(bf).reshape(share, tok_rows, feat)
    slot = lax.rem(me, share)
    parts = []
    for j in range(share):
        perm = []
        for r in range(members):
            for f in range(groups):
                block = r * share + ((f % share) ^ j)
                perm.append((r * groups + f, (f // share) * groups + block))
        parts.append(lax.ppermute(pick(mixed, slot ^ j), ("member", "fsdp"), perm))
    parts = jnp.stack(parts)
    return jnp.concatenate([pick(parts, slot ^ c) for c in range(share)], axis=1)


def solution(mesh):
    placed = (
        P("fsdp", None),
        P("fsdp", None),
        P("fsdp", None),
        P("member", None, "fsdp"),
        P("member", None, "fsdp"),
        P("member", None, "fsdp"),
    )
    return jax.shard_map(
        body, mesh=mesh, in_specs=placed, out_specs=P("fsdp", "member"), check_vma=False
    )
```

```python
import functools

import jax
import jax.numpy as jnp
from jax import lax
from jax.experimental import pallas as pl
from jax.experimental.pallas import tpu as pltpu
from jax.sharding import PartitionSpec as P

WIDTH = 256
HOP = 2
AHEAD = 2
BATCH = 2
VMEM = 62 * 1024 * 1024


def grid_of(size):
    across = 1
    while across * across * 4 <= size:
        across *= 2
    return size // across, across


def begin(src, dst, sem):
    copy = pltpu.make_async_copy(src, dst, sem)
    copy.start()
    return copy


def taker(refs):
    refs = list(refs)

    def take(count=1):
        out = refs[:count]
        del refs[:count]
        return out

    return take


def rows_at(ref, start, width):
    return ref.at[pl.ds(pl.multiple_of(start, 16), width)]


def chain_kernel(cfg, *refs):
    deep, across, width, sums, sums_in, sums_out, back, back_in = cfg
    take = taker(refs)
    (info,) = take()
    if sums:
        gate, up = take(2)
        toks = take(across)
        got = [take(across - 1) for _ in range(deep)]
    came = take(2) if sums_in or back_in else None
    sent = take(2)
    (hid_out,) = take() if back else (None,)
    if sums:
        toks_v, w_v, tok_sem, w_sem = take(4)
    if came:
        came_v, came_sem = take(2)
    sent_v, sent_sem = take(2)
    if back:
        hid_v, hid_sem = take(2)
    place = info[0]
    odd = lax.rem(place, 2)
    wide = 2 * width if sums_out else 0
    in_wide = came[0].shape[1] - (width if back_in else 0) if came else 0
    half = sent[0].shape[0]
    copies = []

    waits = [[], []]
    for s in range(2):
        if came:
            for slot in range(2):

                @pl.when(lax.rem(odd + s, 2) == 1 - slot)
                def _(src=came[slot], s=s):
                    pltpu.make_async_copy(src, came_v.at[s], came_sem.at[s]).start()

            waits[s].append(pltpu.make_async_copy(came[0], came_v.at[s], came_sem.at[s]))
    if sums:
        part_rows = gate.shape[0] // across
        group_rows, feat = toks[0].shape[0], gate.shape[1]
        tok_copies = [[], []]
        for i in list(range(across // 2, across)) + list(range(across // 2)):
            for j in range(across):
                column = pl.multiple_of(jnp.bitwise_xor(info[1], j) * feat, 128)
                tok_copies[i // (across // 2)].append(
                    begin(
                        toks[i].at[:, pl.ds(column, feat)],
                        toks_v.at[j, pl.ds(i * group_rows, group_rows)],
                        tok_sem.at[i, j],
                    )
                )
        for s in range(2):
            own = info[1] * part_rows + info[2 + s]
            for k, ref in enumerate((gate, up)):
                waits[s].append(
                    begin(
                        rows_at(ref, own, width),
                        w_v.at[s, 0, pl.ds(k * width, width)],
                        w_sem.at[s, 0, k],
                    )
                )
            for j in range(1, across):
                dst, sem = w_v.at[s, j], w_sem.at[s, j, 0]
                for i in range(deep):
                    here = i if s == 0 else deep - 1 - i

                    @pl.when(place == here)
                    def _(src=got[i][j - 1], dst=dst, sem=sem):
                        pltpu.make_async_copy(src.at[pl.ds(0, 2 * width)], dst, sem).start()

                waits[s].append(
                    pltpu.make_async_copy(got[0][j - 1].at[pl.ds(0, 2 * width)], dst, sem)
                )

    ends = []
    for s in range(2):
        for copy in waits[s]:
            copy.wait()
        if not sums:
            continue
        mine = 1 - s
        for copy in tok_copies[mine]:
            copy.wait()
        total = None
        for j in range(across):
            term = lax.dot_general(
                toks_v[j, pl.ds(mine * half, half), :],
                w_v[s, j],
                (((1,), (1,)), ((), ())),
                preferred_element_type=jnp.float32,
            )
            total = term if total is None else total + term
        if sums_in:
            first = place == (0 if s == 0 else deep - 1)
            before = came_v[s, :, : 2 * width].astype(jnp.float32)
            total = total + jnp.where(first, 0.0, before)
        if sums_out:
            sent_v[s, :, : 2 * width] = total.astype(jnp.bfloat16)
        if back:
            value, upper = total[:, :width], total[:, width:]
            hidden = value / (1.0 + jnp.exp(-value)) * upper
            column = lax.broadcasted_iota(jnp.int32, hidden.shape, 1)
            ends.append(jnp.where(column >= info[4], hidden, 0.0).astype(jnp.bfloat16))
    if back:
        for s in range(2):
            value = came_v[s, :, in_wide:] if back_in else None
            if sums:
                at_end = place == (0 if s == 0 else deep - 1)
                other = value if back_in else jnp.zeros_like(ends[1 - s])
                value = jnp.where(at_end, ends[1 - s], other)
            sent_v[s, :, wide:] = value
            hid_v[pl.ds(s * half, half)] = value
    for s in range(2):
        for slot in range(2):

            @pl.when(lax.rem(odd + s, 2) == slot)
            def _(dst=sent[slot], s=s):
                pltpu.make_async_copy(sent_v.at[s], dst, sent_sem.at[s]).start()

        copies.append(pltpu.make_async_copy(sent_v.at[s], sent[0], sent_sem.at[s]))
    if back:
        copies.append(begin(hid_v, hid_out, hid_sem))
    for copy in copies:
        copy.wait()


def side_kernel(cfg, *refs):
    deep, across, width, steps_direct, offsets, n_send, kinds = cfg
    steps = len(steps_direct)
    take = taker(refs)
    (info,) = take()
    gate, up, down = take(3)
    hids = [take(2) if direct else take() for direct in steps_direct]
    got = [[take(across - 1) for _ in range(deep)] for _ in range(steps)]
    acc_in = take() if steps else None
    sent = take(n_send)
    acc_out = take() if steps else None
    if n_send:
        send_v, send_sem, sendo_sem = take(3)
    if steps:
        hid_v, d_v, acc_v, hid_sem, d_sem, acc_sem, acco_sem = take(7)
    place = info[0]
    part_rows = gate.shape[0] // across
    waits, copies, sends = [], [], []
    if steps:
        acc_in, acc_out = acc_in[0], acc_out[0]
        half = acc_in.shape[0] // 2
        for n in range(steps):
            for s in range(2):
                here = hid_v.at[n, pl.ds(s * half, half)]
                sem = hid_sem.at[n, s]
                if len(hids[n]) == 1:
                    waits.append(begin(hids[n][0].at[pl.ds(s * half, half)], here, sem))
                    continue
                for slot in range(2):

                    @pl.when(lax.rem(place + s, 2) == 1 - slot)
                    def _(src=hids[n][slot], here=here, sem=sem):
                        pltpu.make_async_copy(src, here, sem).start()

                waits.append(pltpu.make_async_copy(hids[n][0], here, sem))
            for s in range(2):
                own = info[1] * part_rows + info[2 + 4 * n + s]
                waits.append(
                    begin(rows_at(down, own, width), d_v.at[n, s, 0], d_sem.at[n, s, 0])
                )
                for j in range(1, across):
                    dst, sem = d_v.at[n, s, j], d_sem.at[n, s, j]
                    for i in range(deep):
                        here = i if s == 0 else deep - 1 - i

                        @pl.when(place == here)
                        def _(src=got[n][i][j - 1], at=offsets[n][i], dst=dst, sem=sem):
                            pltpu.make_async_copy(src.at[pl.ds(at, width)], dst, sem).start()

                    src = got[n][0][j - 1].at[pl.ds(offsets[n][0], width)]
                    waits.append(pltpu.make_async_copy(src, dst, sem))
        tile = half // 2
        acc_loads = [
            pltpu.make_async_copy(
                acc_in.at[pl.ds(i * tile, tile)], acc_v.at[pl.ds(i * tile, tile)], acc_sem.at[i]
            )
            for i in range(4)
        ]
        acc_stores = [
            pltpu.make_async_copy(
                acc_v.at[pl.ds(i * tile, tile)], acc_out.at[pl.ds(i * tile, tile)], acco_sem.at[i]
            )
            for i in range(4)
        ]
        needed = []
        for s in range(2):
            flags = [info[4 + 4 * n + s] for n in range(steps)]
            needed.append(functools.reduce(jnp.maximum, flags) > 0)

            @pl.when(needed[s])
            def _(s=s):
                for i in (2 * s, 2 * s + 1):
                    acc_loads[i].start()

    base = 2 + 4 * steps
    for j in range(n_send):
        for k, kind in enumerate(kinds):
            ref = (gate, up, down)[kind]
            sends.append(
                begin(
                    rows_at(ref, info[base + 2 * j + kind // 2], width),
                    send_v.at[j, pl.ds(k * width, width)],
                    send_sem.at[j, k],
                )
            )
    for copy in sends:
        copy.wait()
    for j in range(n_send):
        copies.append(begin(send_v.at[j], sent[j], sendo_sem.at[j]))
    if steps:
        for copy in waits:
            copy.wait()
        feat = d_v.shape[-1]
        for s in range(2):

            @pl.when(needed[s])
            def _(s=s):
                for i in (2 * s, 2 * s + 1):
                    here = pl.ds(i * tile, tile)
                    acc_loads[i].wait()
                    for j in range(across):
                        total = acc_v[here, pl.ds(j * feat, feat)]
                        for n in range(steps):
                            hidden = hid_v[n, here, :]
                            valid = info[4 + 4 * n + s] > 0
                            hidden = jnp.where(valid, hidden, jnp.zeros_like(hidden))
                            total += lax.dot_general(
                                hidden,
                                d_v[n, s, j],
                                (((1,), (0,)), ((), ())),
                                preferred_element_type=jnp.float32,
                            )
                        acc_v[here, pl.ds(j * feat, feat)] = total
                    acc_stores[i].start()

        for s in range(2):

            @pl.when(needed[s])
            def _(s=s):
                for i in (2 * s, 2 * s + 1):
                    acc_stores[i].wait()

    for copy in copies:
        copy.wait()


def call(kernel, args, outs, scratch, aliases, flops, nbytes, name):
    return list(
        pl.pallas_call(
            kernel,
            out_shape=outs,
            in_specs=[pl.BlockSpec(memory_space=pltpu.SMEM)]
            + [pl.BlockSpec(memory_space=pl.ANY)] * (len(args) - 1),
            out_specs=[pl.BlockSpec(memory_space=pl.ANY)] * len(outs),
            scratch_shapes=scratch,
            input_output_aliases=aliases,
            compiler_params=pltpu.CompilerParams(vmem_limit_bytes=VMEM),
            cost_estimate=pl.CostEstimate(
                flops=flops, bytes_accessed=nbytes, transcendentals=0
            ),
            name=name,
        )(*args)
    )


def body(tokens, routes, combine, gate_weight, up_weight, down_weight):
    hop, width, ahead, batch = HOP, WIDTH, AHEAD, BATCH
    expert = lax.axis_index("member")
    members = lax.axis_size("member")
    groups = lax.axis_size("fsdp")
    me = lax.axis_index("fsdp")
    deep, across = grid_of(groups)
    z, x = me // across, lax.rem(me, across)
    tok_rows = tokens.shape[0]
    capacity = 3 * tok_rows // members
    gate_weight, up_weight, down_weight = gate_weight[0], up_weight[0], down_weight[0]
    hidden_all, feat = gate_weight.shape
    part_rows = hidden_all // across
    n_chunks = -(-part_rows // width)
    total_rows = capacity * groups
    half_rows = total_rows // 2
    bf, f32 = jnp.bfloat16, jnp.float32
    dma = pltpu.SemaphoreType.DMA

    def swap(array, dz, dx):
        perm = [
            (a * across + b, (a ^ dz) * across + (b ^ dx))
            for a in range(deep)
            for b in range(across)
        ]
        return lax.ppermute(array, "fsdp", perm)

    def pairing(array, slot):
        perm = []
        for m in range(members):
            for a in range(deep):
                b = a ^ 1 if slot == 0 else ((a + 1) ^ 1) - 1
                for c in range(across):
                    there = (m, b) if 0 <= b < deep else (m ^ 1, a)
                    perm.append(
                        (m * groups + a * across + c, there[0] * groups + there[1] * across + c)
                    )
        return lax.ppermute(array, ("member", "fsdp"), perm)

    def start_of(chunk):
        return jnp.minimum(jnp.clip(chunk, 0, n_chunks - 1) * width, part_rows - width)

    got = {}

    def hand_over(k, arrays):
        got[k] = [swap(a, 0, j + 1) for j, a in enumerate(arrays)]

    def send_start(k, j):
        return (x ^ j) * part_rows + min(k * width, part_rows - width)

    reach = hop * (deep - 1)

    def kinds_of(k):
        return (0, 1) * (k < n_chunks) + (2,) * (reach <= k < n_chunks + reach)

    def send_starts(k):
        return [send_start(c, j) for j in range(1, across) for c in (k, max(k - reach, 0))]

    def message(k):
        return [jax.ShapeDtypeStruct((len(kinds_of(k)) * width, feat), bf)] * (across - 1)

    def lay_out(k, weights):
        n_send, rows = across - 1, len(kinds_of(k)) * width
        return call(
            functools.partial(side_kernel, (deep, across, width, (), (), n_send, kinds_of(k))),
            [jnp.stack([z, x] + send_starts(k)).astype(jnp.int32)] + list(weights),
            message(k),
            [pltpu.VMEM((n_send, rows, feat), bf), dma((n_send, 3)), dma((n_send,))],
            {},
            0,
            2 * 1024 * 1024,
            "side_step",
        )

    weights = (gate_weight, up_weight, down_weight)
    early = min(ahead, n_chunks)
    firsts = [lay_out(k, weights) for k in range(early)]
    hand_over(0, firsts[0])

    picked = routes == expert
    chosen = jnp.any(picked, axis=1)
    token_weight = jnp.sum(jnp.where(picked, combine, jnp.zeros_like(combine)), axis=1)
    position = jnp.cumsum(chosen.astype(jnp.int32)) - 1
    slot_ids = jnp.arange(capacity, dtype=jnp.int32)
    placed = (position[:, None] == slot_ids[None, :]) & chosen[:, None]
    packed = lax.dot_general(
        placed.astype(bf), tokens, (((0,), (0,)), ((), ())), preferred_element_type=f32
    ).astype(bf)
    token_ids = jnp.arange(tok_rows, dtype=jnp.int32)
    came_from = jnp.sum(jnp.where(placed, token_ids[:, None] + 1, 0), axis=0)
    weight = jnp.sum(jnp.where(placed, token_weight[:, None], 0.0), axis=0)
    notes = jnp.stack([came_from.astype(f32), weight])

    def pick(array, index):
        return lax.dynamic_index_in_dim(array, index, 0, keepdims=False)

    def columns(array, index, size):
        return lax.dynamic_slice_in_dim(array, index * size, size, 1)

    pieces = []
    for k in range(deep):
        piece = columns(packed, z ^ k, across * feat)
        pieces.append(swap(piece, k, 0) if k else piece)
    pieces = jnp.stack(pieces)
    mine = jnp.concatenate([pick(pieces, z ^ a) for a in range(deep)])
    mine, notes, ready = lax.optimization_barrier((mine, notes, {k: got[k] for k in got}))
    got.update(ready)
    notes = jnp.stack([swap(notes, k, 0) if k else notes for k in range(deep)])
    notes = jnp.stack([pick(notes, z ^ a) for a in range(deep)])
    by_group = [swap(mine, 0, i) if i else mine for i in range(across)]
    by_group, notes, firsts = lax.optimization_barrier((by_group, notes, firsts))
    for k in range(1, early):
        hand_over(k, firsts[k])
    n_steps = n_chunks + 2 * reach
    acc = jnp.zeros((total_rows, across * feat), f32)
    msgs, waiting, order = {}, [], None
    early_at = reach + n_chunks - 1 + hop * (deep // 2 - 1)
    early_half = jnp.where(z < deep // 2, 0, 1)

    def own_parts(which):
        rows = lax.dynamic_slice_in_dim(acc, which * half_rows, half_rows, 0)
        return [
            swap(rows[:, j * feat : (j + 1) * feat].astype(bf), 0, j) for j in range(1, across)
        ]

    last_skip = n_chunks * width - part_rows

    def send_on(t, res):
        if t == n_chunks + reach - 1:
            msgs[t - 1], res = lax.optimization_barrier((msgs[t - 1], res))
        msgs[t] = (pairing(res[0], 0), pairing(res[1], 1))
        if t == n_chunks + reach - 1:
            for u in range(t + 1, n_steps - hop):
                msgs[u] = [pairing(msgs[u - hop][1], 0)] * 2
                if u < n_steps - 2 * hop:
                    msgs[u] = (msgs[u][0], pairing(msgs[u - hop][0], 1))

    def chunks(base):
        return [min(max(base - hop * i, 0), n_chunks - 1) for i in range(deep)]

    for t in range(n_steps):
        sums = t < n_chunks + reach
        back = t >= reach
        if not sums:
            waiting.append((t, msgs[t - hop]))
        if sums:
            before = t - hop
            sums_in = sums and before >= 0
            sums_out = t + hop < n_chunks + reach
            back_in = back and before >= reach
            cfg = (deep, across, width, sums, sums_in, sums_out, back, back_in)
            skip = last_skip if t - reach == n_chunks - 1 else 0
            up_c, dn_c = t - hop * z, t - hop * (deep - 1 - z)
            info = jnp.stack([z, x, start_of(up_c), start_of(dn_c), jnp.int32(skip)]).astype(
                jnp.int32
            )
            if order is not None:
                info, order = lax.optimization_barrier((info, order))
                if "acc" in order:
                    acc = order["acc"]
                if "sent" in order:
                    hand_over(t - 1 + early, order["sent"])
                order = None
            args, outs, scratch = [info], [], []
            if sums:
                args += [gate_weight, up_weight] + by_group + [a for c in chunks(t) for a in got[c]]
                scratch += [
                    pltpu.VMEM((across, total_rows, feat), bf),
                    pltpu.VMEM((2, across, 2 * width, feat), bf),
                    dma((across, across)),
                    dma((2, across, 2)),
                ]
            if sums_in or back_in:
                args += list(msgs[before])
                scratch += [pltpu.VMEM((2,) + msgs[before][0].shape, bf), dma((2,))]
            out_width = 2 * width * sums_out + width * back
            outs += [jax.ShapeDtypeStruct((half_rows, out_width), bf)] * 2
            scratch += [pltpu.VMEM((2, half_rows, out_width), bf), dma((2,))]
            if back:
                outs += [jax.ShapeDtypeStruct((total_rows, width), bf)]
                scratch += [pltpu.VMEM((total_rows, width), bf), dma]
            res = call(
                functools.partial(chain_kernel, cfg),
                args,
                outs,
                scratch,
                {},
                4 * total_rows * width * across * feat * sums,
                8 * 1024 * 1024,
                "chain_step",
            )
            if back:
                waiting.append((t, [res[2]]))

        next_k = t + early
        kinds = kinds_of(next_k)
        n_send = across - 1 if kinds else 0
        flush = len(waiting) == batch and t < early_at
        flush = flush or t in (early_at, n_steps - 1)
        steps = len(waiting) if flush else 0
        if not steps and not n_send:
            if sums:
                send_on(t, res)
            continue
        done, entries = [], [z, x]
        if steps:
            done, waiting = waiting, []
        for at, _ in done:
            up_c, dn_c = at - reach - hop * z, at - reach - hop * (deep - 1 - z)
            entries += [start_of(up_c), start_of(dn_c)]
            entries += [((c >= 0) & (c < n_chunks)).astype(jnp.int32) for c in (up_c, dn_c)]
        if n_send:
            entries += send_starts(next_k)
        side_info = jnp.stack([jnp.int32(e) for e in entries]).astype(jnp.int32)
        if sums:
            side_info, res = lax.optimization_barrier((side_info, res))
            if t == n_chunks + 2:
                notes, res = lax.optimization_barrier((notes, res))
                notes = [swap(notes, 0, i) if i else notes for i in range(across)]
            send_on(t, res)
        if t == n_chunks + reach - 1:
            side_info, msgs[t + hop], got[t] = lax.optimization_barrier(
                (side_info, msgs[t + hop], got[t])
            )
        elif t == early_at:
            late = {u: m for u, m in msgs.items() if u >= n_chunks + reach}
            side_info, notes, late = lax.optimization_barrier((side_info, notes, late))
            msgs.update(late)
        args = [side_info]
        args += [gate_weight, up_weight, down_weight] + [h for _, hid in done for h in hid]
        offsets = []
        for at, _ in done:
            args += [a for c in chunks(at - reach) for a in got[c + reach]]
            offsets.append(
                tuple(2 * width * (c + reach < n_chunks) for c in chunks(at - reach))
            )
        aliases, outs, scratch = {}, [], []
        if n_send:
            outs += message(next_k)
            scratch += [
                pltpu.VMEM((n_send, len(kinds) * width, feat), bf),
                dma((n_send, 3)),
                dma((n_send,)),
            ]
        if steps:
            aliases = {len(args): n_send}
            args += [acc]
            outs += [jax.ShapeDtypeStruct(acc.shape, f32)]
            scratch += [
                pltpu.VMEM((steps, total_rows, width), bf),
                pltpu.VMEM((steps, 2, across, width, feat), bf),
                pltpu.VMEM(acc.shape, f32),
                dma((steps, 2)),
                dma((steps, 2, across)),
                dma((4,)),
                dma((4,)),
            ]
        res = call(
            functools.partial(
                side_kernel,
                (
                    deep,
                    across,
                    width,
                    tuple(len(h) == 2 for _, h in done),
                    tuple(offsets),
                    n_send,
                    kinds,
                ),
            ),
            args,
            outs,
            scratch,
            aliases,
            2 * total_rows * width * across * feat * steps,
            (12 if steps else 2) * 1024 * 1024,
            "side_step",
        )
        order = {}
        if steps:
            order["acc"] = acc = res.pop()
        if n_send:
            order["sent"] = res
        if t == early_at:
            early_parts = own_parts(early_half)

    acc, early_parts = lax.optimization_barrier((acc, early_parts))
    late_parts = own_parts(1 - early_half)
    group_rows = total_rows // across
    whole = acc[:, :feat]
    for j in range(1, across):
        first, second = early_parts[j - 1], late_parts[j - 1]
        part = jnp.concatenate(
            [
                jnp.where(early_half == 0, first, second),
                jnp.where(early_half == 0, second, first),
            ]
        )
        part = jnp.concatenate(
            [part[(i ^ j) * group_rows : ((i ^ j) + 1) * group_rows] for i in range(across)]
        )
        whole = whole + part.astype(f32)
    whole = whole.reshape(across * deep, capacity, feat)
    notes = jnp.concatenate(notes)
    came_from, weight = notes[:, 0].astype(jnp.int32) - 1, notes[:, 1]
    spread = (came_from[:, None, :] == token_ids[None, :, None]).astype(bf)
    high = lax.reduce_precision(whole, 8, 7)
    weighted = sum(
        lax.dot_general(
            spread,
            part.astype(bf),
            (((2,), (1,)), ((0,), (0,))),
            preferred_element_type=f32,
        )
        for part in (high, whole - high)
    )
    row_weight = jnp.sum(
        jnp.where(
            came_from[:, None, :] == token_ids[None, :, None], weight[:, None, :], 0.0
        ),
        axis=2,
    )
    weighted = (weighted * row_weight[:, :, None]).reshape(across, deep, tok_rows, feat)
    weighted = jnp.stack([pick(weighted, x ^ b) for b in range(across)], axis=1)
    share = groups // members
    left = weighted.reshape(members, share * tok_rows, feat)
    bit = 1
    while bit < members:
        pairs = left.reshape(left.shape[0] // 2, 2, share * tok_rows, feat)
        side = (expert // bit) % 2
        keep, give = (
            lax.dynamic_index_in_dim(pairs, s, 1, keepdims=False) for s in (side, 1 - side)
        )
        give = give if bit == 1 else give.astype(bf)
        came = lax.ppermute(give, "member", [(m, m ^ bit) for m in range(members)])
        left = keep + came.astype(f32)
        bit *= 2
    mixed = left.astype(bf).reshape(share, tok_rows, feat)
    slot = lax.rem(me, share)
    parts = []
    for j in range(share):
        perm = []
        for r in range(members):
            for f in range(groups):
                block = r * share + ((f % share) ^ j)
                perm.append((r * groups + f, (f // share) * groups + block))
        parts.append(lax.ppermute(pick(mixed, slot ^ j), ("member", "fsdp"), perm))
    parts = jnp.stack(parts)
    return jnp.concatenate([pick(parts, slot ^ c) for c in range(share)], axis=1)


def solution(mesh):
    placed = (
        P("fsdp", None),
        P("fsdp", None),
        P("fsdp", None),
        P("member", None, "fsdp"),
        P("member", None, "fsdp"),
        P("member", None, "fsdp"),
    )
    return jax.shard_map(
        body, mesh=mesh, in_specs=placed, out_specs=P("fsdp", "member"), check_vma=False
    )
```

```python
import functools

import jax
import jax.numpy as jnp
from jax import lax
from jax.experimental import pallas as pl
from jax.experimental.pallas import tpu as pltpu
from jax.sharding import PartitionSpec as P

WIDTH = 256
HOP = 2
AHEAD = 2
BATCH = 2
VMEM = 62 * 1024 * 1024


def grid_of(size):
    across = 1
    while across * across * 4 <= size:
        across *= 2
    return size // across, across


def begin(src, dst, sem):
    copy = pltpu.make_async_copy(src, dst, sem)
    copy.start()
    return copy


def taker(refs):
    refs = list(refs)

    def take(count=1):
        out = refs[:count]
        del refs[:count]
        return out

    return take


def rows_at(ref, start, width):
    return ref.at[pl.ds(pl.multiple_of(start, 16), width)]


def chain_kernel(cfg, *refs):
    deep, across, width, sums, sums_in, sums_out, back, back_in = cfg
    take = taker(refs)
    (info,) = take()
    if sums:
        gate, up = take(2)
        toks = take(across)
        got = [take(across - 1) for _ in range(deep)]
    came = take(2) if sums_in or back_in else None
    sent = take(2)
    (hid_out,) = take() if back else (None,)
    if sums:
        toks_v, w_v, tok_sem, w_sem = take(4)
    if came:
        came_v, came_sem = take(2)
    sent_v, sent_sem = take(2)
    if back:
        hid_v, hid_sem = take(2)
    place = info[0]
    odd = lax.rem(place, 2)
    wide = 2 * width if sums_out else 0
    in_wide = came[0].shape[1] - (width if back_in else 0) if came else 0
    half = sent[0].shape[0]
    copies = []

    waits = [[], []]
    for s in range(2):
        if came:
            for slot in range(2):

                @pl.when(lax.rem(odd + s, 2) == 1 - slot)
                def _(src=came[slot], s=s):
                    pltpu.make_async_copy(src, came_v.at[s], came_sem.at[s]).start()

            waits[s].append(pltpu.make_async_copy(came[0], came_v.at[s], came_sem.at[s]))
    if sums:
        part_rows = gate.shape[0] // across
        group_rows, feat = toks[0].shape[0], gate.shape[1]
        tok_copies = [[], []]
        for i in list(range(across // 2, across)) + list(range(across // 2)):
            for j in range(across):
                column = pl.multiple_of(jnp.bitwise_xor(info[1], j) * feat, 128)
                tok_copies[i // (across // 2)].append(
                    begin(
                        toks[i].at[:, pl.ds(column, feat)],
                        toks_v.at[j, pl.ds(i * group_rows, group_rows)],
                        tok_sem.at[i, j],
                    )
                )
        for s in range(2):
            own = info[1] * part_rows + info[2 + s]
            for k, ref in enumerate((gate, up)):
                waits[s].append(
                    begin(
                        rows_at(ref, own, width),
                        w_v.at[s, 0, pl.ds(k * width, width)],
                        w_sem.at[s, 0, k],
                    )
                )
            for j in range(1, across):
                dst, sem = w_v.at[s, j], w_sem.at[s, j, 0]
                for i in range(deep):
                    here = i if s == 0 else deep - 1 - i

                    @pl.when(place == here)
                    def _(src=got[i][j - 1], dst=dst, sem=sem):
                        pltpu.make_async_copy(src.at[pl.ds(0, 2 * width)], dst, sem).start()

                waits[s].append(
                    pltpu.make_async_copy(got[0][j - 1].at[pl.ds(0, 2 * width)], dst, sem)
                )

    ends = []
    for s in range(2):
        for copy in waits[s]:
            copy.wait()
        if not sums:
            continue
        mine = 1 - s
        for copy in tok_copies[mine]:
            copy.wait()
        total = None
        for j in range(across):
            term = lax.dot_general(
                toks_v[j, pl.ds(mine * half, half), :],
                w_v[s, j],
                (((1,), (1,)), ((), ())),
                preferred_element_type=jnp.float32,
            )
            total = term if total is None else total + term
        if sums_in:
            first = place == (0 if s == 0 else deep - 1)
            before = came_v[s, :, : 2 * width].astype(jnp.float32)
            total = total + jnp.where(first, 0.0, before)
        if sums_out:
            sent_v[s, :, : 2 * width] = total.astype(jnp.bfloat16)
        if back:
            value, upper = total[:, :width], total[:, width:]
            hidden = value / (1.0 + jnp.exp(-value)) * upper
            column = lax.broadcasted_iota(jnp.int32, hidden.shape, 1)
            ends.append(jnp.where(column >= info[4], hidden, 0.0).astype(jnp.bfloat16))
    if back:
        for s in range(2):
            value = came_v[s, :, in_wide:] if back_in else None
            if sums:
                at_end = place == (0 if s == 0 else deep - 1)
                other = value if back_in else jnp.zeros_like(ends[1 - s])
                value = jnp.where(at_end, ends[1 - s], other)
            sent_v[s, :, wide:] = value
            hid_v[pl.ds(s * half, half)] = value
    for s in range(2):
        for slot in range(2):

            @pl.when(lax.rem(odd + s, 2) == slot)
            def _(dst=sent[slot], s=s):
                pltpu.make_async_copy(sent_v.at[s], dst, sent_sem.at[s]).start()

        copies.append(pltpu.make_async_copy(sent_v.at[s], sent[0], sent_sem.at[s]))
    if back:
        copies.append(begin(hid_v, hid_out, hid_sem))
    for copy in copies:
        copy.wait()


def side_kernel(cfg, *refs):
    deep, across, width, steps_direct, offsets, n_send, kinds = cfg
    steps = len(steps_direct)
    take = taker(refs)
    (info,) = take()
    gate, up, down = take(3)
    hids = [take(2) if direct else take() for direct in steps_direct]
    got = [[take(across - 1) for _ in range(deep)] for _ in range(steps)]
    acc_in = take() if steps else None
    sent = take(n_send)
    acc_out = take() if steps else None
    if n_send:
        send_v, send_sem, sendo_sem = take(3)
    if steps:
        hid_v, d_v, acc_v, hid_sem, d_sem, acc_sem, acco_sem = take(7)
    place = info[0]
    part_rows = gate.shape[0] // across
    waits, copies, sends = [], [], []
    if steps:
        acc_in, acc_out = acc_in[0], acc_out[0]
        half = acc_in.shape[0] // 2
        for n in range(steps):
            for s in range(2):
                here = hid_v.at[n, pl.ds(s * half, half)]
                sem = hid_sem.at[n, s]
                if len(hids[n]) == 1:
                    waits.append(begin(hids[n][0].at[pl.ds(s * half, half)], here, sem))
                    continue
                for slot in range(2):

                    @pl.when(lax.rem(place + s, 2) == 1 - slot)
                    def _(src=hids[n][slot], here=here, sem=sem):
                        pltpu.make_async_copy(src, here, sem).start()

                waits.append(pltpu.make_async_copy(hids[n][0], here, sem))
            for s in range(2):
                own = info[1] * part_rows + info[2 + 4 * n + s]
                waits.append(
                    begin(rows_at(down, own, width), d_v.at[n, s, 0], d_sem.at[n, s, 0])
                )
                for j in range(1, across):
                    dst, sem = d_v.at[n, s, j], d_sem.at[n, s, j]
                    for i in range(deep):
                        here = i if s == 0 else deep - 1 - i

                        @pl.when(place == here)
                        def _(src=got[n][i][j - 1], at=offsets[n][i], dst=dst, sem=sem):
                            pltpu.make_async_copy(src.at[pl.ds(at, width)], dst, sem).start()

                    src = got[n][0][j - 1].at[pl.ds(offsets[n][0], width)]
                    waits.append(pltpu.make_async_copy(src, dst, sem))
        tile = half // 2
        acc_loads = [
            pltpu.make_async_copy(
                acc_in.at[pl.ds(i * tile, tile)], acc_v.at[pl.ds(i * tile, tile)], acc_sem.at[i]
            )
            for i in range(4)
        ]
        acc_stores = [
            pltpu.make_async_copy(
                acc_v.at[pl.ds(i * tile, tile)], acc_out.at[pl.ds(i * tile, tile)], acco_sem.at[i]
            )
            for i in range(4)
        ]
        needed = []
        for s in range(2):
            flags = [info[4 + 4 * n + s] for n in range(steps)]
            needed.append(functools.reduce(jnp.maximum, flags) > 0)

            @pl.when(needed[s])
            def _(s=s):
                for i in (2 * s, 2 * s + 1):
                    acc_loads[i].start()

    base = 2 + 4 * steps
    for j in range(n_send):
        for k, kind in enumerate(kinds):
            ref = (gate, up, down)[kind]
            sends.append(
                begin(
                    rows_at(ref, info[base + 2 * j + kind // 2], width),
                    send_v.at[j, pl.ds(k * width, width)],
                    send_sem.at[j, k],
                )
            )
    for copy in sends:
        copy.wait()
    for j in range(n_send):
        copies.append(begin(send_v.at[j], sent[j], sendo_sem.at[j]))
    if steps:
        for copy in waits:
            copy.wait()
        feat = d_v.shape[-1]
        for s in range(2):

            @pl.when(needed[s])
            def _(s=s):
                for i in (2 * s, 2 * s + 1):
                    here = pl.ds(i * tile, tile)
                    acc_loads[i].wait()
                    for j in range(across):
                        total = acc_v[here, pl.ds(j * feat, feat)]
                        for n in range(steps):
                            hidden = hid_v[n, here, :]
                            valid = info[4 + 4 * n + s] > 0
                            hidden = jnp.where(valid, hidden, jnp.zeros_like(hidden))
                            total += lax.dot_general(
                                hidden,
                                d_v[n, s, j],
                                (((1,), (0,)), ((), ())),
                                preferred_element_type=jnp.float32,
                            )
                        acc_v[here, pl.ds(j * feat, feat)] = total
                    acc_stores[i].start()

        for s in range(2):

            @pl.when(needed[s])
            def _(s=s):
                for i in (2 * s, 2 * s + 1):
                    acc_stores[i].wait()

    for copy in copies:
        copy.wait()


def call(kernel, args, outs, scratch, aliases, flops, nbytes, name):
    return list(
        pl.pallas_call(
            kernel,
            out_shape=outs,
            in_specs=[pl.BlockSpec(memory_space=pltpu.SMEM)]
            + [pl.BlockSpec(memory_space=pl.ANY)] * (len(args) - 1),
            out_specs=[pl.BlockSpec(memory_space=pl.ANY)] * len(outs),
            scratch_shapes=scratch,
            input_output_aliases=aliases,
            compiler_params=pltpu.CompilerParams(vmem_limit_bytes=VMEM),
            cost_estimate=pl.CostEstimate(
                flops=flops, bytes_accessed=nbytes, transcendentals=0
            ),
            name=name,
        )(*args)
    )


def body(tokens, routes, combine, gate_weight, up_weight, down_weight):
    hop, width, ahead, batch = HOP, WIDTH, AHEAD, BATCH
    expert = lax.axis_index("member")
    members = lax.axis_size("member")
    groups = lax.axis_size("fsdp")
    me = lax.axis_index("fsdp")
    deep, across = grid_of(groups)
    z, x = me // across, lax.rem(me, across)
    tok_rows = tokens.shape[0]
    capacity = 3 * tok_rows // members
    gate_weight, up_weight, down_weight = gate_weight[0], up_weight[0], down_weight[0]
    hidden_all, feat = gate_weight.shape
    part_rows = hidden_all // across
    n_chunks = -(-part_rows // width)
    total_rows = capacity * groups
    half_rows = total_rows // 2
    bf, f32 = jnp.bfloat16, jnp.float32
    dma = pltpu.SemaphoreType.DMA

    def swap(array, dz, dx):
        perm = [
            (a * across + b, (a ^ dz) * across + (b ^ dx))
            for a in range(deep)
            for b in range(across)
        ]
        return lax.ppermute(array, "fsdp", perm)

    def pairing(array, slot):
        perm = []
        for m in range(members):
            for a in range(deep):
                b = a ^ 1 if slot == 0 else ((a + 1) ^ 1) - 1
                for c in range(across):
                    there = (m, b) if 0 <= b < deep else (m ^ 1, a)
                    perm.append(
                        (m * groups + a * across + c, there[0] * groups + there[1] * across + c)
                    )
        return lax.ppermute(array, ("member", "fsdp"), perm)

    def start_of(chunk):
        return jnp.minimum(jnp.clip(chunk, 0, n_chunks - 1) * width, part_rows - width)

    got = {}

    def hand_over(k, arrays):
        got[k] = [swap(a, 0, j + 1) for j, a in enumerate(arrays)]

    def send_start(k, j):
        return (x ^ j) * part_rows + min(k * width, part_rows - width)

    reach = hop * (deep - 1)

    def kinds_of(k):
        return (0, 1) * (k < n_chunks) + (2,) * (reach <= k < n_chunks + reach)

    def send_starts(k):
        return [send_start(c, j) for j in range(1, across) for c in (k, max(k - reach, 0))]

    def message(k):
        return [jax.ShapeDtypeStruct((len(kinds_of(k)) * width, feat), bf)] * (across - 1)

    def lay_out(k, weights):
        n_send, rows = across - 1, len(kinds_of(k)) * width
        return call(
            functools.partial(side_kernel, (deep, across, width, (), (), n_send, kinds_of(k))),
            [jnp.stack([z, x] + send_starts(k)).astype(jnp.int32)] + list(weights),
            message(k),
            [pltpu.VMEM((n_send, rows, feat), bf), dma((n_send, 3)), dma((n_send,))],
            {},
            0,
            2 * 1024 * 1024,
            "side_step",
        )

    weights = (gate_weight, up_weight, down_weight)
    early = min(ahead, n_chunks)

    picked = routes == expert
    chosen = jnp.any(picked, axis=1)
    token_weight = jnp.sum(jnp.where(picked, combine, jnp.zeros_like(combine)), axis=1)
    position = jnp.cumsum(chosen.astype(jnp.int32)) - 1
    slot_ids = jnp.arange(capacity, dtype=jnp.int32)
    placed = (position[:, None] == slot_ids[None, :]) & chosen[:, None]
    packed = lax.dot_general(
        placed.astype(bf), tokens, (((0,), (0,)), ((), ())), preferred_element_type=f32
    ).astype(bf)
    token_ids = jnp.arange(tok_rows, dtype=jnp.int32)
    came_from = jnp.sum(jnp.where(placed, token_ids[:, None] + 1, 0), axis=0)
    weight = jnp.sum(jnp.where(placed, token_weight[:, None], 0.0), axis=0)
    notes = jnp.stack([came_from.astype(f32), weight])

    def pick(array, index):
        return lax.dynamic_index_in_dim(array, index, 0, keepdims=False)

    def columns(array, index, size):
        return lax.dynamic_slice_in_dim(array, index * size, size, 1)

    packed, weights = lax.optimization_barrier((packed, weights))
    firsts = [lay_out(k, weights) for k in range(early)]
    hand_over(0, firsts[0])
    pieces = []
    for k in range(deep):
        piece = columns(packed, z ^ k, across * feat)
        pieces.append(swap(piece, k, 0) if k else piece)
    pieces = jnp.stack(pieces)
    mine = jnp.concatenate([pick(pieces, z ^ a) for a in range(deep)])
    mine, notes, ready = lax.optimization_barrier((mine, notes, {k: got[k] for k in got}))
    got.update(ready)
    notes = jnp.stack([swap(notes, k, 0) if k else notes for k in range(deep)])
    notes = jnp.stack([pick(notes, z ^ a) for a in range(deep)])
    by_group = [swap(mine, 0, i) if i else mine for i in range(across)]
    by_group, notes, firsts = lax.optimization_barrier((by_group, notes, firsts))
    for k in range(1, early):
        hand_over(k, firsts[k])
    n_steps = n_chunks + 2 * reach
    acc = jnp.zeros((total_rows, across * feat), f32)
    msgs, waiting, order = {}, [], None
    early_at = reach + n_chunks - 1 + hop * (deep // 2 - 1)
    early_half = jnp.where(z < deep // 2, 0, 1)

    def own_parts(which):
        rows = lax.dynamic_slice_in_dim(acc, which * half_rows, half_rows, 0)
        return [
            swap(rows[:, j * feat : (j + 1) * feat].astype(bf), 0, j) for j in range(1, across)
        ]

    last_skip = n_chunks * width - part_rows

    def send_on(t, res):
        if t == n_chunks + reach - 1:
            msgs[t - 1], res = lax.optimization_barrier((msgs[t - 1], res))
        msgs[t] = (pairing(res[0], 0), pairing(res[1], 1))
        if t == n_chunks + reach - 1:
            for u in range(t + 1, n_steps - hop):
                msgs[u] = [pairing(msgs[u - hop][1], 0)] * 2
                if u < n_steps - 2 * hop:
                    msgs[u] = (msgs[u][0], pairing(msgs[u - hop][0], 1))

    def chunks(base):
        return [min(max(base - hop * i, 0), n_chunks - 1) for i in range(deep)]

    for t in range(n_steps):
        sums = t < n_chunks + reach
        back = t >= reach
        if not sums:
            waiting.append((t, msgs[t - hop]))
        if sums:
            before = t - hop
            sums_in = sums and before >= 0
            sums_out = t + hop < n_chunks + reach
            back_in = back and before >= reach
            cfg = (deep, across, width, sums, sums_in, sums_out, back, back_in)
            skip = last_skip if t - reach == n_chunks - 1 else 0
            up_c, dn_c = t - hop * z, t - hop * (deep - 1 - z)
            info = jnp.stack([z, x, start_of(up_c), start_of(dn_c), jnp.int32(skip)]).astype(
                jnp.int32
            )
            if order is not None:
                info, order = lax.optimization_barrier((info, order))
                if "acc" in order:
                    acc = order["acc"]
                if "sent" in order:
                    hand_over(t - 1 + early, order["sent"])
                order = None
            args, outs, scratch = [info], [], []
            if sums:
                args += [gate_weight, up_weight] + by_group + [a for c in chunks(t) for a in got[c]]
                scratch += [
                    pltpu.VMEM((across, total_rows, feat), bf),
                    pltpu.VMEM((2, across, 2 * width, feat), bf),
                    dma((across, across)),
                    dma((2, across, 2)),
                ]
            if sums_in or back_in:
                args += list(msgs[before])
                scratch += [pltpu.VMEM((2,) + msgs[before][0].shape, bf), dma((2,))]
            out_width = 2 * width * sums_out + width * back
            outs += [jax.ShapeDtypeStruct((half_rows, out_width), bf)] * 2
            scratch += [pltpu.VMEM((2, half_rows, out_width), bf), dma((2,))]
            if back:
                outs += [jax.ShapeDtypeStruct((total_rows, width), bf)]
                scratch += [pltpu.VMEM((total_rows, width), bf), dma]
            res = call(
                functools.partial(chain_kernel, cfg),
                args,
                outs,
                scratch,
                {},
                4 * total_rows * width * across * feat * sums,
                8 * 1024 * 1024,
                "chain_step",
            )
            if back:
                waiting.append((t, [res[2]]))

        next_k = t + early
        kinds = kinds_of(next_k)
        n_send = across - 1 if kinds else 0
        flush = len(waiting) == batch and t < early_at
        flush = flush or t in (early_at, n_steps - 1)
        steps = len(waiting) if flush else 0
        if not steps and not n_send:
            if sums:
                send_on(t, res)
            continue
        done, entries = [], [z, x]
        if steps:
            done, waiting = waiting, []
        for at, _ in done:
            up_c, dn_c = at - reach - hop * z, at - reach - hop * (deep - 1 - z)
            entries += [start_of(up_c), start_of(dn_c)]
            entries += [((c >= 0) & (c < n_chunks)).astype(jnp.int32) for c in (up_c, dn_c)]
        if n_send:
            entries += send_starts(next_k)
        side_info = jnp.stack([jnp.int32(e) for e in entries]).astype(jnp.int32)
        if sums:
            side_info, res = lax.optimization_barrier((side_info, res))
            if t == n_chunks + 2:
                notes, res = lax.optimization_barrier((notes, res))
                notes = [swap(notes, 0, i) if i else notes for i in range(across)]
            send_on(t, res)
        if t == n_chunks + reach - 1:
            side_info, msgs[t + hop], got[t] = lax.optimization_barrier(
                (side_info, msgs[t + hop], got[t])
            )
        elif t == early_at:
            late = {u: m for u, m in msgs.items() if u >= n_chunks + reach}
            side_info, notes, late = lax.optimization_barrier((side_info, notes, late))
            msgs.update(late)
        args = [side_info]
        args += [gate_weight, up_weight, down_weight] + [h for _, hid in done for h in hid]
        offsets = []
        for at, _ in done:
            args += [a for c in chunks(at - reach) for a in got[c + reach]]
            offsets.append(
                tuple(2 * width * (c + reach < n_chunks) for c in chunks(at - reach))
            )
        aliases, outs, scratch = {}, [], []
        if n_send:
            outs += message(next_k)
            scratch += [
                pltpu.VMEM((n_send, len(kinds) * width, feat), bf),
                dma((n_send, 3)),
                dma((n_send,)),
            ]
        if steps:
            aliases = {len(args): n_send}
            args += [acc]
            outs += [jax.ShapeDtypeStruct(acc.shape, f32)]
            scratch += [
                pltpu.VMEM((steps, total_rows, width), bf),
                pltpu.VMEM((steps, 2, across, width, feat), bf),
                pltpu.VMEM(acc.shape, f32),
                dma((steps, 2)),
                dma((steps, 2, across)),
                dma((4,)),
                dma((4,)),
            ]
        res = call(
            functools.partial(
                side_kernel,
                (
                    deep,
                    across,
                    width,
                    tuple(len(h) == 2 for _, h in done),
                    tuple(offsets),
                    n_send,
                    kinds,
                ),
            ),
            args,
            outs,
            scratch,
            aliases,
            2 * total_rows * width * across * feat * steps,
            (12 if steps else 2) * 1024 * 1024,
            "side_step",
        )
        order = {}
        if steps:
            order["acc"] = acc = res.pop()
        if n_send:
            order["sent"] = res
        if t == early_at:
            early_parts = own_parts(early_half)

    acc, early_parts = lax.optimization_barrier((acc, early_parts))
    late_parts = own_parts(1 - early_half)
    group_rows = total_rows // across
    whole = acc[:, :feat]
    for j in range(1, across):
        first, second = early_parts[j - 1], late_parts[j - 1]
        part = jnp.concatenate(
            [
                jnp.where(early_half == 0, first, second),
                jnp.where(early_half == 0, second, first),
            ]
        )
        part = jnp.concatenate(
            [part[(i ^ j) * group_rows : ((i ^ j) + 1) * group_rows] for i in range(across)]
        )
        whole = whole + part.astype(f32)
    whole = whole.reshape(across * deep, capacity, feat)
    notes = jnp.concatenate(notes)
    came_from, weight = notes[:, 0].astype(jnp.int32) - 1, notes[:, 1]
    spread = (came_from[:, None, :] == token_ids[None, :, None]).astype(bf)
    high = lax.reduce_precision(whole, 8, 7)
    weighted = sum(
        lax.dot_general(
            spread,
            part.astype(bf),
            (((2,), (1,)), ((0,), (0,))),
            preferred_element_type=f32,
        )
        for part in (high, whole - high)
    )
    row_weight = jnp.sum(
        jnp.where(
            came_from[:, None, :] == token_ids[None, :, None], weight[:, None, :], 0.0
        ),
        axis=2,
    )
    weighted = (weighted * row_weight[:, :, None]).reshape(across, deep, tok_rows, feat)
    weighted = jnp.stack([pick(weighted, x ^ b) for b in range(across)], axis=1)
    share = groups // members
    left = weighted.reshape(members, share * tok_rows, feat)
    bit = 1
    while bit < members:
        pairs = left.reshape(left.shape[0] // 2, 2, share * tok_rows, feat)
        side = (expert // bit) % 2
        keep, give = (
            lax.dynamic_index_in_dim(pairs, s, 1, keepdims=False) for s in (side, 1 - side)
        )
        give = give if bit == 1 else give.astype(bf)
        came = lax.ppermute(give, "member", [(m, m ^ bit) for m in range(members)])
        left = keep + came.astype(f32)
        bit *= 2
    mixed = left.astype(bf).reshape(share, tok_rows, feat)
    slot = lax.rem(me, share)
    parts = []
    for j in range(share):
        perm = []
        for r in range(members):
            for f in range(groups):
                block = r * share + ((f % share) ^ j)
                perm.append((r * groups + f, (f // share) * groups + block))
        parts.append(lax.ppermute(pick(mixed, slot ^ j), ("member", "fsdp"), perm))
    parts = jnp.stack(parts)
    return jnp.concatenate([pick(parts, slot ^ c) for c in range(share)], axis=1)


def solution(mesh):
    placed = (
        P("fsdp", None),
        P("fsdp", None),
        P("fsdp", None),
        P("member", None, "fsdp"),
        P("member", None, "fsdp"),
        P("member", None, "fsdp"),
    )
    return jax.shard_map(
        body, mesh=mesh, in_specs=placed, out_specs=P("fsdp", "member"), check_vma=False
    )
```
